256 devices in a mesh: ctx: 32 (over z, x), head: 8 (over y, core).
Axes of the slice: x: 4, y: 4, z: 8, core: 2. Of those that a mesh axis runs over, the one named last changes fastest.
Arguments:
- queries: bfloat16 [256, 128, 192], P('ctx', 'head'), may hold values from -135 to 135
- absorb_k: bfloat16 [128, 128, 512], P('head'), may hold values from -0.5 to 0.5
- absorb_v: bfloat16 [128, 512, 128], P('head'), may hold values from -1.5 to 1.5
- cache: bfloat16 [32768, 576], P(('ctx', 'head')), may hold values from -4 to 4
- new_entries: bfloat16 [256, 576], P('ctx'), may hold values from -5 to 5
- cache_len: int32 [1], replicated, may hold values from 16384 to 32768
Outputs:
- attended: bfloat16 [256, 128, 128], P('ctx', 'head')
The draws below stay inside these ranges and needn't reach their ends.
All inputs are finite; a program needn't handle non-finite values.
Results may differ from the reference program's by a relative error of at most 0.0077.
Values may be sent and summed in bfloat16 or wider, within the bound.
A program may use at most 128 MiB of HBM per device.

```python
import math
import jax
import jax.numpy as jnp
from jax import lax

HEADS = 128
NOPE = 128
ROPE = 64
LATENT = 512
VDIM = 128
ROWS_DEV = 8
SPAN = 256
CACHE = 32768
N_CTX = 32


def draw_queries(key, part):
    key = jax.random.fold_in(key, 1)
    qk_width = NOPE + ROPE
    return (2.6 * jax.random.truncated_normal(key, -4.0, 4.0, (SPAN, HEADS, qk_width), jnp.float32)).astype(jnp.bfloat16)


def draw_cache(key, part):
    key = jax.random.fold_in(key, 2)
    key_width = LATENT + ROPE
    return jax.random.truncated_normal(key, -4.0, 4.0, (CACHE, key_width), jnp.float32).astype(jnp.bfloat16)


def level_of(stream_key, extent, shards, low, top_value):
    loudness = 1.0
    for position, parts in shards:
        heights = jax.random.uniform(jax.random.fold_in(jax.random.fold_in(stream_key, 6), position), (parts,), jnp.float32, low / len(shards), top_value / len(shards))
        loudness = loudness * jnp.repeat(jnp.exp(heights), extent[position] // parts).reshape((-1,) + (1,) * (len(extent) - 1 - position))
    return loudness


def normal_values(rng, shape, spread, most, split=(), held_as=jnp.bfloat16):
    drawn = jax.random.normal(rng, shape, jnp.float32) * spread
    if len(split) > 0:
        drawn = level_of(rng, shape, split, -0.22, 0.18) * drawn
    return jnp.clip(drawn, min=-most, max=most).astype(held_as)


def setup_inputs(seed: int = 0) -> dict:
    key_of = jax.random.split(jax.random.key(seed), 7)
    queries = draw_queries(jax.random.fold_in(key_of[6], 71), 0)
    absorb_k = normal_values(key_of[1], (HEADS, NOPE, LATENT), NOPE ** -0.5, 0.5, ((0, 8),))
    absorb_v = normal_values(key_of[2], (HEADS, LATENT, VDIM), (max(LATENT // 32, 1)) ** -0.5, 1.5, ((0, 8),))
    cache = draw_cache(jax.random.fold_in(key_of[6], 71), 0)
    new_entries = normal_values(key_of[4], (SPAN, LATENT + ROPE), 1.0, 5.0, ((0, 32),))
    cache_len = jax.random.randint(key_of[5], (1,), CACHE // 2, CACHE + 1).astype(jnp.int32)
    return dict(queries=queries, absorb_k=absorb_k, absorb_v=absorb_v, cache=cache, new_entries=new_entries, cache_len=cache_len)


def reference(queries, absorb_k, absorb_v, cache, new_entries, cache_len):
    qk_width = NOPE + ROPE
    row_ids = jnp.arange(SPAN, dtype=jnp.int32)
    ranks = row_ids % ROWS_DEV * N_CTX + row_ids // ROWS_DEV
    slot_ok = jnp.arange(CACHE, dtype=jnp.int32) < cache_len[0]
    new_ok = ranks[None, :] <= ranks[:, None]
    is_valid = jnp.concatenate([jnp.broadcast_to(slot_ok[None, :], (SPAN, CACHE)), new_ok], axis=1)
    all_keys = jnp.concatenate([cache, new_entries], axis=0)
    values = all_keys[:, :LATENT]

    def one_head(operands):
        head_q, head_k, head_v = operands
        lat_q = jnp.dot(head_q[:, :NOPE], head_k, preferred_element_type=jnp.float32).astype(jnp.bfloat16)
        absorbed = jnp.concatenate([lat_q, head_q[:, NOPE:]], axis=1)
        scores = jnp.dot(absorbed, all_keys.T, preferred_element_type=jnp.float32) / math.sqrt(qk_width)
        scores = jnp.where(is_valid, scores, -1e+30)
        row_top = lax.optimization_barrier(jnp.max(scores, axis=1, keepdims=True))
        weights = jnp.where(is_valid, jnp.exp(scores - row_top), 0.0)
        total = lax.optimization_barrier(jnp.sum(weights, axis=1, keepdims=True))
        mixed = jnp.dot(weights.astype(jnp.bfloat16), values, preferred_element_type=jnp.float32)
        latent_out = mixed / total
        return jnp.dot(latent_out, head_v.astype(jnp.float32), precision=lax.Precision.HIGHEST, preferred_element_type=jnp.float32).astype(jnp.bfloat16)
    outputs = lax.map(one_head, (jnp.transpose(queries, (1, 0, 2)), absorb_k, absorb_v))
    return jnp.transpose(outputs, (1, 0, 2))
```

```python
import math

import jax
import jax.numpy as jnp
from jax import lax
from jax.experimental import pallas as pl
from jax.experimental.pallas import tpu as pltpu
from jax.sharding import PartitionSpec as P

f32 = jnp.float32
bf16 = jnp.bfloat16
NEG = -1e30
LOG2E = 1.4426950408889634
MESH = pl.DeviceIdType.MESH

NZ, NX, NY = 8, 4, 4
BLK = 128
WIDE = 640
LAT = 512
NEW_ROWS = 64
CH = 4 * BLK
FIRST = NEW_ROWS + CH
ROWS = 1024

ORDER = [
    (0, 0, 0), (1, 0, 0), (0, 1, 0), (0, 2, 0),
    (0, 0, 1), (0, 0, 2), (1, 1, 0), (1, 2, 0),
    (1, 0, 1), (1, 0, 2), (0, 3, 0), (0, 0, 3),
    (0, 1, 1), (0, 1, 2), (0, 2, 1), (0, 2, 2),
    (1, 3, 0), (1, 0, 3), (1, 1, 1), (1, 1, 2),
    (1, 2, 1), (1, 2, 2), (0, 3, 1), (0, 3, 2),
    (0, 1, 3), (0, 2, 3), (1, 3, 1), (1, 3, 2),
    (1, 1, 3), (1, 2, 3), (0, 3, 3), (1, 3, 3),
]
PLACE = {b: NEW_ROWS + BLK * n for n, b in enumerate(ORDER)}


def dot_t(a, b):
    return lax.dot_general(a, b, (((1,), (1,)), ((), ())), preferred_element_type=f32)


def dot_n(a, b):
    return jnp.dot(a, b, preferred_element_type=f32)


def kernel(
    scale, q_ref, cache_ref, new_ref, len_ref, wk_hbm, wv_hbm, out_ref,
    kbuf, nsend, qsend, qrecv, qabs, qn, wk, wv, sa, sb, pa, pb, al, top, tot, acc, ob, osend, orecv, ssend, srecv,
    w_sem, send_sem, k_sem, s_sem, q_sem, n_sem, o_sem, t_sem,
):
    ctx = lax.axis_index("ctx")
    head = lax.axis_index("head")
    z, x = ctx // NX, ctx % NX
    y, c = head // 2, head % 2

    def at(zz, xx, yy, cc):
        return (zz * NX + xx, yy * 2 + cc)

    step1x, step1y = 1 - c, c
    ax1p = at(z, (x + step1x) % NX, (y + step1y) % NY, c)
    ax1m = at(z, (x + 3 * step1x) % NX, (y + 3 * step1y) % NY, c)
    ax2p = at(z, (x + step1y) % NX, (y + step1x) % NY, c)
    ax2m = at(z, (x + 3 * step1y) % NX, (y + 3 * step1x) % NY, c)
    sib = at(z, x, y, 1 - c)
    z_to = [None] + [at((z + d) % NZ, x, y, c) for d in range(1, NZ)]
    z_back = [None] + [at((z + NZ - d) % NZ, x, y, c) for d in range(1, NZ)]
    x_to = [None] + [at(z, (x + d) % NX, y, c) for d in range(1, NX)]

    wk_copy = pltpu.make_async_copy(wk_hbm, wk, w_sem.at[0])
    wv_copy = pltpu.make_async_copy(wv_hbm, wv, w_sem.at[1])
    wk_copy.start()
    wv_copy.start()

    barrier = pltpu.get_barrier_semaphore()
    partners = [ax1p, ax1m, ax2p, ax2m, sib] + z_to[1:] + x_to[1:]
    for who in partners:
        pl.semaphore_signal(barrier, inc=1, device_id=who, device_id_type=MESH)

    length = len_ref[0]
    own = PLACE[(0, 0, 0)]
    slot = ctx * (NY * 2 * BLK) + head * BLK + lax.broadcasted_iota(jnp.int32, (BLK, 64), 0)
    bias = jnp.where(slot < length, 0.0, NEG).astype(bf16)
    kbuf[own : own + BLK, 0:LAT] = cache_ref[:, 0:LAT]
    kbuf[own : own + BLK, LAT:WIDE] = jnp.concatenate([cache_ref[:, LAT:576], bias], axis=1)
    qsend[0:128, :] = q_ref[:, 0:128]
    qsend[128:192, :] = jnp.concatenate([q_ref[0:64, 128:192], q_ref[64:128, 128:192]], axis=1)
    fresh = new_ref[...].astype(f32)
    fresh = jnp.concatenate([fresh, jnp.zeros((8, 576), f32)], axis=0)
    fresh = jnp.concatenate([fresh, jnp.zeros((16, 64), f32)], axis=1).astype(bf16)
    kbuf[0:16, :] = fresh
    nsend[...] = fresh

    pl.semaphore_wait(barrier, len(partners))

    sent = {}

    def send(key, src, dst, who, recv):
        number = sent[key][0] if key in sent else len(sent)
        copy = pltpu.make_async_remote_copy(
            src_ref=src, dst_ref=dst, send_sem=send_sem.at[number], recv_sem=recv, device_id=who, device_id_type=MESH
        )
        sent[key] = (number, src)
        copy.start()

    def rows_of(block, half=None):
        lo = PLACE[block]
        if half is None:
            return kbuf.at[lo : lo + BLK]
        return kbuf.at[lo + 64 * half : lo + 64 * half + 64]

    def k_send(block, to_block, who, half=None):
        _, d1, d2 = to_block
        key = ("k", to_block, half)
        send(key, rows_of(block, half), rows_of(to_block, half), who, k_sem.at[d1 * 4 + d2, half or 0])

    def sib_send(d1, d2):
        send(("s", d1, d2), rows_of((0, d1, d2)), rows_of((1, d1, d2)), sib, s_sem.at[d1 * 4 + d2])

    def wait_at(ref, sem):
        pltpu.make_async_copy(ref, ref, sem).wait()

    def wait_sib(d1, d2):
        wait_at(rows_of((1, d1, d2)), s_sem.at[d1 * 4 + d2])

    def event(d1, d2):
        block = (0, d1, d2)
        sem = d1 * 4 + d2
        if d2 == 3 or (d1, d2) == (3, 0):
            wait_at(rows_of(block, 0), k_sem.at[sem, 0])
            wait_at(rows_of(block, 1), k_sem.at[sem, 1])
        else:
            wait_at(rows_of(block), k_sem.at[sem, 0])
        if d2 == 0:
            if d1 == 1:
                k_send(block, (0, 3, 0), ax1p, 0)
            if d1 == 2:
                k_send(block, (0, 3, 0), ax1m, 1)
            k_send(block, (0, d1, 1), ax2p)
            k_send(block, (0, d1, 2), ax2m)
        elif d2 == 1:
            k_send(block, (0, d1, 3), ax2p, 0)
        elif d2 == 2:
            k_send(block, (0, d1, 3), ax2m, 1)
        sib_send(d1, d2)

    for d in (1, 7, 2, 6, 3, 5, 4):
        send(("q", d), qsend, qrecv.at[d], z_to[d], q_sem.at[d])
    mine = (0, 0, 0)
    k_send(mine, (0, 1, 0), ax1p)
    k_send(mine, (0, 2, 0), ax1m)
    k_send(mine, (0, 0, 1), ax2p)
    k_send(mine, (0, 0, 2), ax2m)
    sib_send(0, 0)
    for d in range(1, NX):
        send(("n", d), nsend, kbuf.at[16 * d : 16 * d + 16], x_to[d], n_sem.at[d])

    event(1, 0)
    event(2, 0)
    event(0, 1)
    event(0, 2)

    lane64 = lax.broadcasted_iota(jnp.int32, (128, 64), 1)
    row_j = lax.broadcasted_iota(jnp.int32, (128, 64), 0) // 16
    for d in range(NZ):
        if d:
            wait_at(qrecv.at[d], q_sem.at[d])
        block = qsend if d == 0 else qrecv.at[d]
        at_d = slice(128 * d, 128 * d + 128)
        qn[at_d, :] = block[0:128, :].astype(f32)
        rope = block[128:192, :]
        rope = jnp.concatenate([rope[:, 0:64], rope[:, 64:128]], axis=0)
        pick = jnp.where(lane64 == d * 8 + row_j, 1.0, 0.0).astype(bf16)
        qabs[at_d, LAT:WIDE] = jnp.concatenate([rope, pick], axis=1)
    event(3, 0)
    wk_copy.wait()
    for h in range(16):
        part = qn[pl.ds(h, 64, stride=16), :].astype(bf16)
        lat = dot_n(part, wk[h])
        for n in range(4):
            acc[n, pl.ds(h, 64, stride=16), :] = lat[:, 128 * n : 128 * n + 128]
    for t in range(16):
        r = slice(64 * t, 64 * t + 64)
        for n in range(4):
            qabs[r, 128 * n : 128 * n + 128] = acc[n, r, :].astype(bf16)

    for d in range(1, NX):
        wait_at(kbuf.at[16 * d : 16 * d + 16], n_sem.at[d])
    tail = kbuf[0:NEW_ROWS, LAT:WIDE].astype(f32)
    n_row = lax.broadcasted_iota(jnp.int32, (NEW_ROWS, 128), 0)
    col = lax.broadcasted_iota(jnp.int32, (NEW_ROWS, 128), 1) - 64
    n_j = n_row % 16
    n_rank = n_j * (NZ * NX) + z * NX + (x + NX - n_row // 16) % NX
    q_rank = (col % 8) * (NZ * NX) + (z + NZ - col // 8) % NZ * NX + x
    n_bias = jnp.where((n_j < 8) & (n_rank <= q_rank), 0.0, NEG)
    kbuf[0:NEW_ROWS, LAT:WIDE] = jnp.where(col >= 0, n_bias, tail).astype(bf16)

    event(1, 1)
    event(1, 2)
    event(2, 1)
    event(2, 2)
    event(0, 3)

    def scores(base, size, s):
        for lo in range(0, size, 256):
            n = min(256, size - lo)
            k = kbuf[pl.ds(base + lo, n), :]
            s[:, lo : lo + n] = dot_t(qabs[...], k)

    def weigh(size, s, p, first):
        for t in range(ROWS // 32):
            r = slice(32 * t, 32 * t + 32)
            sc = s[r, 0:size]
            new_top = jnp.broadcast_to(jnp.max(sc, axis=1, keepdims=True), (32, 128))
            if not first:
                old_top = top[r, :]
                new_top = jnp.maximum(old_top, new_top)
                shrink = jnp.exp2((old_top - new_top) * scale)
                al[r, :] = shrink
            top[r, :] = new_top
            w = jnp.exp2((sc - new_top[:, 0:1]) * scale)
            part = w[:, 0:128]
            for lo in range(128, CH, 128):
                part = part + w[:, lo : lo + 128]
            if size > CH:
                part = part + jnp.concatenate([w[:, CH:size], jnp.zeros((32, 128 - (size - CH)), f32)], axis=1)
            if not first:
                part = part + tot[r, :] * shrink
            tot[r, :] = part
            p[r, 0:size] = w.astype(bf16)

    def mix(base, size, p, first):
        for n in range(2):
            v = kbuf[pl.ds(base, size), 256 * n : 256 * n + 256]
            for t in range(ROWS // 256):
                r = slice(256 * t, 256 * t + 256)
                o = dot_n(p[r, 0:size], v)
                for k in range(2):
                    part = o[:, 128 * k : 128 * k + 128]
                    m = 2 * n + k
                    acc[m, r, :] = part if first else acc[m, r, :] * al[r, :] + part

    def base_of(step):
        return pl.multiple_of(NEW_ROWS + step * CH, 64)

    wait_sib(0, 0)
    scores(0, FIRST, sa)
    for d in ((1, 0), (2, 0)):
        wait_sib(*d)
    scores(base_of(1), CH, sb)
    weigh(FIRST, sa, pa, True)
    mix(0, FIRST, pa, True)
    event(3, 1)
    event(3, 2)

    def arrive(step):
        if step == 1:
            wait_sib(0, 1)
            wait_sib(0, 2)
        elif step == 2:
            event(1, 3)
            event(2, 3)
        elif step == 3:
            event(3, 3)
            for d in ((3, 0), (0, 3), (1, 1), (1, 2)):
                wait_sib(*d)
        elif step == 4:
            wait_sib(2, 1)
            wait_sib(2, 2)
        elif step == 5:
            wait_sib(3, 1)
            wait_sib(3, 2)
        else:
            wait_sib(1, 3)
            wait_sib(2, 3)
            wait_sib(3, 3)

    def pair(g, carry):
        for k in range(2):
            for gg in range(3):
                pl.when(g == gg)(lambda step=1 + 2 * gg + k: arrive(step))
            step = 1 + 2 * g + k
            s_now, s_next, p = (sb, sa, pb) if k == 0 else (sa, sb, pa)
            scores(base_of(step + 1), CH, s_next)
            weigh(CH, s_now, p, False)
            mix(base_of(step), CH, p, False)
        return carry

    lax.fori_loop(0, 3, pair, 0)
    weigh(CH, sb, pb, False)
    mix(base_of(7), CH, pb, False)

    lane = lax.broadcasted_iota(jnp.int32, (128, 128), 1)
    for d in range(NZ):
        r = slice(128 * d, 128 * d + 128)
        total = jnp.sum(tot[r, :], axis=1, keepdims=True)
        ssend[d] = jnp.where(lane == 0, top[r, :], total).T[0:8, :]
        if d:
            send(("t", d), ssend.at[d], srecv.at[d], z_back[d], t_sem.at[d])
    wv_copy.wait()
    for h in range(16):
        part = jnp.concatenate([acc[n, pl.ds(h, 64, stride=16), :] for n in range(4)], axis=1)
        hi = part.astype(bf16)
        lo = (part - hi.astype(f32)).astype(bf16)
        both = dot_n(jnp.concatenate([hi, lo], axis=0), wv[h])
        ob[pl.ds(h, 64, stride=16), :] = both[0:64] + both[64:128]
    for d in range(1, NZ):
        osend[d] = ob[128 * d : 128 * d + 128, :].astype(bf16)
        send(("o", d), osend.at[d], orecv.at[d], z_back[d], o_sem.at[d])

    for d in range(1, NZ):
        wait_at(srecv.at[d], t_sem.at[d])
    tops = [ssend[0, 0:1, :]] + [srecv[d, 0:1, :] for d in range(1, NZ)]
    totals = [ssend[0, 1:2, :]] + [srecv[d, 1:2, :] for d in range(1, NZ)]
    best = tops[0]
    for d in range(1, NZ):
        best = jnp.maximum(best, tops[d])
    shares = [jnp.exp2((t - best) * scale) for t in tops]
    full = shares[0] * totals[0]
    for d in range(1, NZ):
        full = full + shares[d] * totals[d]
    shares = [s / full for s in shares]
    by_row = jnp.concatenate(shares + [jnp.zeros((120, 128), f32)], axis=0).T
    result = ob[0:128, :] * by_row[:, 0:1]
    for d in range(1, NZ):
        wait_at(orecv.at[d], o_sem.at[d])
        result = result + orecv[d].astype(f32) * by_row[:, d : d + 1]
    out_ref[...] = result.astype(bf16)
    for number, src in sent.values():
        pltpu.make_async_copy(src, src, send_sem.at[number]).wait()


def body(queries, absorb_k, absorb_v, cache, new_entries, cache_len):
    scale = LOG2E / math.sqrt(queries.shape[2])
    vmem = pl.BlockSpec(memory_space=pltpu.VMEM)
    hbm = pl.BlockSpec(memory_space=pl.ANY)
    dma = pltpu.SemaphoreType.DMA

    def run(*refs):
        kernel(scale, *refs)

    out = pl.pallas_call(
        run,
        out_shape=jax.ShapeDtypeStruct((128, 128), bf16),
        in_specs=[vmem, vmem, vmem, pl.BlockSpec(memory_space=pltpu.SMEM), hbm, hbm],
        out_specs=vmem,
        scratch_shapes=[
            pltpu.VMEM((NEW_ROWS + 32 * BLK, WIDE), bf16),
            pltpu.VMEM((16, WIDE), bf16),
            pltpu.VMEM((192, 128), bf16),
            pltpu.VMEM((NZ, 192, 128), bf16),
            pltpu.VMEM((ROWS, WIDE), bf16),
            pltpu.VMEM((ROWS, 128), f32),
            pltpu.VMEM((16, 128, LAT), bf16),
            pltpu.VMEM((16, LAT, 128), bf16),
            pltpu.VMEM((ROWS, WIDE), f32),
            pltpu.VMEM((ROWS, CH), f32),
            pltpu.VMEM((ROWS, WIDE), bf16),
            pltpu.VMEM((ROWS, CH), bf16),
            pltpu.VMEM((ROWS, 128), f32),
            pltpu.VMEM((ROWS, 128), f32),
            pltpu.VMEM((ROWS, 128), f32),
            pltpu.VMEM((4, ROWS, 128), f32),
            pltpu.VMEM((ROWS, 128), f32),
            pltpu.VMEM((NZ, 128, 128), bf16),
            pltpu.VMEM((NZ, 128, 128), bf16),
            pltpu.VMEM((NZ, 8, 128), f32),
            pltpu.VMEM((NZ, 8, 128), f32),
            dma((2,)),
            dma((80,)),
            dma((16, 2)),
            dma((16,)),
            dma((NZ,)),
            dma((NX,)),
            dma((NZ,)),
            dma((NZ,)),
        ],
        compiler_params=pltpu.CompilerParams(
            collective_id=0, has_side_effects=True, vmem_limit_bytes=56 << 20
        ),
    )(queries.reshape(128, 192), cache, new_entries, cache_len, absorb_k, absorb_v)
    return out.reshape(8, 16, 128)


def solution(mesh):
    in_specs = (
        P("ctx", "head", None),
        P("head", None, None),
        P("head", None, None),
        P(("ctx", "head"), None),
        P("ctx", None),
        P(),
    )
    out_specs = P("ctx", "head", None)
    return jax.shard_map(body, mesh=mesh, in_specs=in_specs, out_specs=out_specs, check_vma=False)
```

```python
import math

import jax
import jax.numpy as jnp
from jax import lax
from jax.experimental import pallas as pl
from jax.experimental.pallas import tpu as pltpu
from jax.sharding import PartitionSpec as P

f32 = jnp.float32
bf16 = jnp.bfloat16
NEG = -1e30
LOG2E = 1.4426950408889634
MESH = pl.DeviceIdType.MESH

NZ, NX, NY = 8, 4, 4
BLK = 128
PACK = 144
LAT = 512
NEW_ROWS = 64
CH = 4 * BLK
HALF = 512
ROWS = 2 * HALF

NEAR = (0, 1, 7, 2)
FAR = (6, 3, 5, 4)
SPOT = {d: n for n, d in enumerate(NEAR + FAR)}

ORDER = [
    (0, 0, 0), (1, 0, 0), (0, 1, 0), (0, 2, 0),
    (0, 0, 1), (0, 0, 2), (1, 1, 0), (1, 2, 0),
    (1, 0, 1), (1, 0, 2), (0, 3, 0), (0, 0, 3),
    (0, 1, 1), (0, 1, 2), (0, 2, 1), (0, 2, 2),
    (1, 3, 0), (1, 0, 3), (1, 1, 1), (1, 1, 2),
    (1, 2, 1), (1, 2, 2), (0, 3, 1), (0, 3, 2),
    (0, 1, 3), (0, 2, 3), (1, 3, 1), (1, 3, 2),
    (1, 1, 3), (1, 2, 3), (0, 3, 3), (1, 3, 3),
]
PLACE = {b: n for n, b in enumerate(ORDER)}
OFFSET = (0, 3, 1, 2)

N, F = 0, 1
UNITS = [
    (N, 0), (N, 1), (F, 0), (F, 1), (N, 2), (F, 2), (N, 3), (F, 3),
    (N, 4), (F, 4), (N, 5), (F, 5), (F, 6), (F, 7), (N, 6), (N, 7),
]
PASS = {
    0: [(1, 0), (2, 0), (0, 1), (0, 2)],
    4: [(3, 0), (0, 3), (1, 1), (1, 2), (2, 1), (2, 2)],
    8: [(3, 1), (3, 2)],
    10: [(1, 3), (2, 3)],
    12: [(3, 3)],
}


def dot_t(a, b):
    return lax.dot_general(a, b, (((1,), (1,)), ((), ())), preferred_element_type=f32)


def dot_n(a, b):
    return jnp.dot(a, b, preferred_element_type=f32)


def kernel(
    scale, q_ref, cache_ref, new_ref, len_ref, wk_hbm, wv_hbm, out_ref,
    kbuf, ktail, nsend, nbuf, qsend, qrecv, qabs, qn, wk, wv, sa, sb, pa, pb, al, top, tot, acc, ob, osend, orecv, ssend, srecv,
    w_sem, send_sem, k_sem, s_sem, q_sem, n_sem, o_sem, t_sem,
):
    ctx = lax.axis_index("ctx")
    head = lax.axis_index("head")
    z, x = ctx // NX, ctx % NX
    y, c = head // 2, head % 2

    def at(zz, xx, yy, cc):
        return (zz * NX + xx, yy * 2 + cc)

    on_x, on_y = 1 - c, c
    ax1p = at(z, (x + on_x) % NX, (y + on_y) % NY, c)
    ax1m = at(z, (x + 3 * on_x) % NX, (y + 3 * on_y) % NY, c)
    ax2p = at(z, (x + on_y) % NX, (y + on_x) % NY, c)
    ax2m = at(z, (x + 3 * on_y) % NX, (y + 3 * on_x) % NY, c)
    sib = at(z, x, y, 1 - c)
    z_to = [None] + [at((z + d) % NZ, x, y, c) for d in range(1, NZ)]
    x_to = [None] + [at(z, (x + d) % NX, y, c) for d in range(1, NX)]

    wk_copy = pltpu.make_async_copy(wk_hbm, wk, w_sem.at[0])
    wv_copy = pltpu.make_async_copy(wv_hbm, wv, w_sem.at[1])
    wk_copy.start()
    wv_copy.start()

    barrier = pltpu.get_barrier_semaphore()
    partners = [ax1p, ax1m, ax2p, ax2m, sib] + z_to[1:] + x_to[1:]
    for who in partners:
        pl.semaphore_signal(barrier, inc=1, device_id=who, device_id_type=MESH)

    length = len_ref[0]
    mine = kbuf.at[0]
    qsend[0:128, :] = q_ref[:, 0:128]
    qsend[128:192, :] = jnp.concatenate([q_ref[0:64, 128:192], q_ref[64:128, 128:192]], axis=1)
    for n in range(4):
        mine[0:128, 128 * n : 128 * n + 128] = cache_ref[128 * n : 128 * n + 128, :].astype(f32).T.astype(bf16)
    rope = jnp.concatenate([cache_ref[LAT:576, :].astype(f32), jnp.zeros((64, 128), f32)], axis=0).T
    mine[128:144, :] = jnp.concatenate([rope[16 * g : 16 * g + 16, 0:64] for g in range(8)], axis=1).astype(bf16)
    fresh = new_ref[...].astype(f32)
    fresh = jnp.concatenate([fresh, jnp.zeros((8, 576), f32)], axis=0)
    fresh = jnp.concatenate([fresh, jnp.zeros((16, 64), f32)], axis=1).astype(bf16)
    nbuf[0] = fresh
    nsend[...] = fresh

    pl.semaphore_wait(barrier, len(partners))

    sent = {}

    def send(key, src, dst, who, recv):
        number = len(sent)
        copy = pltpu.make_async_remote_copy(
            src_ref=src, dst_ref=dst, send_sem=send_sem.at[number], recv_sem=recv, device_id=who, device_id_type=MESH
        )
        sent[key] = (number, src)
        copy.start()

    def rows_of(block, half=None):
        ref = kbuf.at[PLACE[block]]
        return ref if half is None else ref.at[0:80] if half == 0 else ref.at[80:144]

    def k_send(block, to_block, who, half=None):
        _, d1, d2 = to_block
        key = ("k", to_block, half)
        send(key, rows_of(block, half), rows_of(to_block, half), who, k_sem.at[d1 * 4 + d2, half or 0])

    def sib_send(d1, d2):
        send(("s", d1, d2), rows_of((0, d1, d2)), rows_of((1, d1, d2)), sib, s_sem.at[d1 * 4 + d2])

    def wait_at(ref, sem):
        pltpu.make_async_copy(ref, ref, sem).wait()

    def wait_sib(d1, d2):
        wait_at(rows_of((1, d1, d2)), s_sem.at[d1 * 4 + d2])

    def event(d1, d2):
        block = (0, d1, d2)
        sem = d1 * 4 + d2
        if d2 == 3 or (d1, d2) == (3, 0):
            wait_at(rows_of(block, 0), k_sem.at[sem, 0])
            wait_at(rows_of(block, 1), k_sem.at[sem, 1])
        else:
            wait_at(rows_of(block), k_sem.at[sem, 0])
        if d2 == 0:
            if d1 == 1:
                k_send(block, (0, 3, 0), ax1p, 0)
            if d1 == 2:
                k_send(block, (0, 3, 0), ax1m, 1)
            k_send(block, (0, d1, 1), ax2p)
            k_send(block, (0, d1, 2), ax2m)
        elif d2 == 1:
            k_send(block, (0, d1, 3), ax2p, 0)
        elif d2 == 2:
            k_send(block, (0, d1, 3), ax2m, 1)
        sib_send(d1, d2)

    def q_send(d, to, half=None, src=None):
        part = slice(0, 192) if half is None else slice(96 * half, 96 * half + 96)
        src = qsend if src is None else src
        send(("q", d, half), src.at[part], qrecv.at[d, part], to, q_sem.at[d, half or 0])

    q_send(1, z_to[1])
    q_send(7, z_to[7])
    q_send(2, z_to[2])
    q_send(6, z_to[6])
    own = (0, 0, 0)
    k_send(own, (0, 1, 0), ax1p)
    k_send(own, (0, 2, 0), ax1m)
    k_send(own, (0, 0, 1), ax2p)
    k_send(own, (0, 0, 2), ax2m)
    sib_send(0, 0)
    for d in range(1, NX):
        send(("n", d), nsend, nbuf.at[d], x_to[d], n_sem.at[d])

    def place(d):
        r = slice(128 * SPOT[d], 128 * SPOT[d] + 128)
        lane64 = lax.broadcasted_iota(jnp.int32, (128, 64), 1)
        row_j = lax.broadcasted_iota(jnp.int32, (128, 64), 0) // 16
        block = qsend if d == 0 else qrecv.at[d]
        qn[r, :] = block[0:128, :].astype(f32)
        rope = block[128:192, :]
        rope = jnp.concatenate([rope[:, 0:64], rope[:, 64:128]], axis=0)
        pick = jnp.where(lane64 == d * 8 + row_j, 1.0, 0.0).astype(bf16)
        qabs[r, LAT:640] = jnp.concatenate([rope, pick], axis=1)

    def absorb(half):
        for h in range(16):
            part = qn[pl.ds(HALF * half + h, 32, stride=16), :].astype(bf16)
            lat = dot_n(part, wk[h])
            for n in range(4):
                acc[n, pl.ds(HALF * half + h, 32, stride=16), :] = lat[:, 128 * n : 128 * n + 128]
        for t in range(8):
            r = slice(HALF * half + 64 * t, HALF * half + 64 * t + 64)
            for n in range(4):
                qabs[r, 128 * n : 128 * n + 128] = acc[n, r, :].astype(bf16)

    def unpack(block):
        plane, d1, d2 = block
        first_x = on_x if plane == 0 else on_y
        s1, s2 = OFFSET[d1], OFFSET[d2]
        sx = (x + s1 * first_x + s2 * (1 - first_x)) % NX
        sy = (y + s1 * (1 - first_x) + s2 * first_x) % NY
        sc = c if plane == 0 else 1 - c
        slot = ((z * NX + sx) * NY + sy) * (2 * BLK) + sc * BLK
        here = PLACE[block]
        packed = kbuf[here, 128:144, :].astype(f32)
        row = lax.broadcasted_iota(jnp.int32, (16, 128), 0)
        lane = lax.broadcasted_iota(jnp.int32, (16, 128), 1)
        for g in range(8):
            piece = packed[:, 128 * (g // 2) : 128 * (g // 2) + 128]
            if g % 2:
                piece = pltpu.roll(piece, 64, 1)
            bias = jnp.where(slot + 16 * g + row < length, 0.0, NEG)
            ktail[BLK * here + 16 * g : BLK * here + 16 * g + 16, :] = jnp.where(lane < 64, piece, bias).astype(bf16)

    def mask_new():
        for d in range(1, NX):
            wait_at(nbuf.at[d], n_sem.at[d])
        n_j = lax.broadcasted_iota(jnp.int32, (16, 128), 0)
        col = lax.broadcasted_iota(jnp.int32, (16, 128), 1) - 64
        q_rank = (col % 8) * (NZ * NX) + (z + NZ - col // 8) % NZ * NX + x
        for d in range(NX):
            n_rank = n_j * (NZ * NX) + z * NX + (x + NX - d) % NX
            bias = jnp.where((n_j < 8) & (n_rank <= q_rank), 0.0, NEG)
            tail = nbuf[d, :, LAT:640].astype(f32)
            nbuf[d, :, LAT:640] = jnp.where(col >= 0, bias, tail).astype(bf16)

    def keys_of(chunk, lo):
        if lo == CH:
            return jnp.concatenate([nbuf[d] for d in range(NX)], axis=0)
        b = chunk * 4 + lo // BLK
        lat = jnp.concatenate([kbuf[b, 0:128, :], kbuf[b + 1, 0:128, :]], axis=0)
        return jnp.concatenate([lat, ktail[BLK * b : BLK * b + 256, :]], axis=1)

    def scores(unit, s):
        half, chunk = unit
        q = qabs.at[HALF * half : HALF * half + HALF]
        for lo in range(0, CH, 256):
            s[:, lo : lo + 256] = dot_t(q[...], keys_of(chunk, lo))
        if chunk == 0:
            s[:, CH : CH + NEW_ROWS] = dot_t(q[...], keys_of(chunk, CH))

    def weigh(unit, s, p):
        half, chunk = unit
        size = CH + NEW_ROWS if chunk == 0 else CH
        for t in range(HALF // 32):
            sr = slice(32 * t, 32 * t + 32)
            r = slice(HALF * half + 32 * t, HALF * half + 32 * t + 32)
            sc = s[sr, 0:size]
            new_top = jnp.broadcast_to(jnp.max(sc, axis=1, keepdims=True), (32, 128))
            if chunk:
                old_top = top[r, :]
                new_top = jnp.maximum(old_top, new_top)
                shrink = jnp.exp2((old_top - new_top) * scale)
                al[sr, :] = shrink
            top[r, :] = new_top
            w = jnp.exp2((sc - new_top[:, 0:1]) * scale)
            part = w[:, 0:128]
            for lo in range(128, CH, 128):
                part = part + w[:, lo : lo + 128]
            if size > CH:
                part = part + jnp.concatenate([w[:, CH:size], jnp.zeros((32, 128 - NEW_ROWS), f32)], axis=1)
            if chunk:
                part = part + tot[r, :] * shrink
            tot[r, :] = part
            p[sr, 0:size] = w.astype(bf16)

    def mix(unit, p):
        half, chunk = unit
        size = CH + NEW_ROWS if chunk == 0 else CH
        for n in range(2):
            cols = slice(256 * n, 256 * n + 256)
            v = [kbuf[chunk * 4 + b, 0:128, cols] for b in range(4)]
            if chunk == 0:
                v = v + [nbuf[d, :, cols] for d in range(NX)]
            v = jnp.concatenate(v, axis=0)
            for t in range(HALF // 256):
                sr = slice(256 * t, 256 * t + 256)
                r = slice(HALF * half + 256 * t, HALF * half + 256 * t + 256)
                o = dot_n(p[sr, 0:size], v)
                for k in range(2):
                    part = o[:, 128 * k : 128 * k + 128]
                    m = 2 * n + k
                    acc[m, r, :] = part if chunk == 0 else acc[m, r, :] * al[sr, :] + part

    def deliver(half):
        lane = lax.broadcasted_iota(jnp.int32, (128, 128), 1)
        owners = NEAR if half == N else FAR
        for d in owners:
            r = slice(128 * SPOT[d], 128 * SPOT[d] + 128)
            total = jnp.sum(tot[r, :], axis=1, keepdims=True)
            ssend[d] = jnp.where(lane == 0, top[r, :], total).T[0:8, :]
            if d:
                send(("t", d), ssend.at[d], srecv.at[d], z_to[NZ - d], t_sem.at[d])
        for h in range(16):
            rows = pl.ds(HALF * half + h, 32, stride=16)
            part = jnp.concatenate([acc[n, rows, :] for n in range(4)], axis=1)
            hi = part.astype(bf16)
            lo = (part - hi.astype(f32)).astype(bf16)
            both = dot_n(jnp.concatenate([hi, lo], axis=0), wv[h])
            ob[rows, :] = both[0:32] + both[32:64]
        for d in owners:
            if d:
                osend[d] = ob[128 * SPOT[d] : 128 * SPOT[d] + 128, :].astype(bf16)
                send(("o", d), osend.at[d], orecv.at[d], z_to[NZ - d], o_sem.at[d])

    def take_near():
        place(0)
        wait_at(qrecv.at[2], q_sem.at[2, 0])
        q_send(3, z_to[1], src=qrecv.at[2])
        q_send(4, z_to[2], half=0, src=qrecv.at[2])
        wait_at(qrecv.at[6], q_sem.at[6, 0])
        q_send(5, z_to[7], src=qrecv.at[6])
        q_send(4, z_to[6], half=1, src=qrecv.at[6])
        wait_at(qrecv.at[1], q_sem.at[1, 0])
        wait_at(qrecv.at[7], q_sem.at[7, 0])
        for d in NEAR[1:]:
            place(d)

    def take_far():
        wait_at(qrecv.at[3], q_sem.at[3, 0])
        wait_at(qrecv.at[5], q_sem.at[5, 0])
        wait_at(qrecv.at[4, 0:96], q_sem.at[4, 0])
        wait_at(qrecv.at[4, 96:192], q_sem.at[4, 1])
        for d in FAR:
            place(d)

    ready = set()
    sib_in = set()

    def before(n):
        half, chunk = UNITS[n]
        if n == 0:
            take_near()
            wk_copy.wait()
            absorb(N)
        for b in PASS.get(n, ()):
            event(*b)
        if (half, chunk) == (F, 0):
            take_far()
            absorb(F)
        if n == 0:
            mask_new()
        if chunk in ready:
            return
        ready.add(chunk)
        for b in ORDER[4 * chunk : 4 * chunk + 4]:
            if b[0] == 1:
                wait_sib(*b[1:])
            unpack(b)

    before(0)
    scores(UNITS[0], sa)
    for n, unit in enumerate(UNITS):
        s_now, s_next, p = (sa, sb, pa) if n % 2 == 0 else (sb, sa, pb)
        if n + 1 < len(UNITS):
            before(n + 1)
            scores(UNITS[n + 1], s_next)
        weigh(unit, s_now, p)
        mix(unit, p)
        if unit == (F, 7):
            wv_copy.wait()
            deliver(F)
    deliver(N)

    for d in range(1, NZ):
        wait_at(srecv.at[d], t_sem.at[d])
    tops = [ssend[0, 0:1, :]] + [srecv[d, 0:1, :] for d in range(1, NZ)]
    totals = [ssend[0, 1:2, :]] + [srecv[d, 1:2, :] for d in range(1, NZ)]
    best = tops[0]
    for d in range(1, NZ):
        best = jnp.maximum(best, tops[d])
    shares = [jnp.exp2((t - best) * scale) for t in tops]
    full = shares[0] * totals[0]
    for d in range(1, NZ):
        full = full + shares[d] * totals[d]
    shares = [s / full for s in shares]
    by_row = jnp.concatenate(shares + [jnp.zeros((120, 128), f32)], axis=0).T
    result = ob[0:128, :] * by_row[:, 0:1]
    for d in FAR + NEAR[1:]:
        wait_at(orecv.at[d], o_sem.at[d])
        result = result + orecv[d].astype(f32) * by_row[:, d : d + 1]
    out_ref[...] = result.astype(bf16)
    for number, src in sent.values():
        pltpu.make_async_copy(src, src, send_sem.at[number]).wait()


def body(queries, absorb_k, absorb_v, cache, new_entries, cache_len):
    scale = LOG2E / math.sqrt(queries.shape[2])
    vmem = pl.BlockSpec(memory_space=pltpu.VMEM)
    hbm = pl.BlockSpec(memory_space=pl.ANY)
    dma = pltpu.SemaphoreType.DMA

    def run(*refs):
        kernel(scale, *refs)

    out = pl.pallas_call(
        run,
        out_shape=jax.ShapeDtypeStruct((128, 128), bf16),
        in_specs=[vmem, vmem, vmem, pl.BlockSpec(memory_space=pltpu.SMEM), hbm, hbm],
        out_specs=vmem,
        scratch_shapes=[
            pltpu.VMEM((32, PACK, LAT), bf16),
            pltpu.VMEM((32 * BLK, 128), bf16),
            pltpu.VMEM((16, 640), bf16),
            pltpu.VMEM((NX, 16, 640), bf16),
            pltpu.VMEM((192, 128), bf16),
            pltpu.VMEM((NZ, 192, 128), bf16),
            pltpu.VMEM((ROWS, 640), bf16),
            pltpu.VMEM((ROWS, 128), f32),
            pltpu.VMEM((16, 128, LAT), bf16),
            pltpu.VMEM((16, LAT, 128), bf16),
            pltpu.VMEM((HALF, 640), f32),
            pltpu.VMEM((HALF, 640), f32),
            pltpu.VMEM((HALF, 640), bf16),
            pltpu.VMEM((HALF, 640), bf16),
            pltpu.VMEM((HALF, 128), f32),
            pltpu.VMEM((ROWS, 128), f32),
            pltpu.VMEM((ROWS, 128), f32),
            pltpu.VMEM((4, ROWS, 128), f32),
            pltpu.VMEM((ROWS, 128), f32),
            pltpu.VMEM((NZ, 128, 128), bf16),
            pltpu.VMEM((NZ, 128, 128), bf16),
            pltpu.VMEM((NZ, 8, 128), f32),
            pltpu.VMEM((NZ, 8, 128), f32),
            dma((2,)),
            dma((88,)),
            dma((16, 2)),
            dma((16,)),
            dma((NZ, 2)),
            dma((NX,)),
            dma((NZ,)),
            dma((NZ,)),
        ],
        compiler_params=pltpu.CompilerParams(
            collective_id=0, has_side_effects=True, vmem_limit_bytes=56 << 20
        ),
    )(queries.reshape(128, 192), cache.T, new_entries, cache_len, absorb_k, absorb_v)
    return out.reshape(8, 16, 128)


def solution(mesh):
    in_specs = (
        P("ctx", "head", None),
        P("head", None, None),
        P("head", None, None),
        P(("ctx", "head"), None),
        P("ctx", None),
        P(),
    )
    out_specs = P("ctx", "head", None)
    return jax.shard_map(body, mesh=mesh, in_specs=in_specs, out_specs=out_specs, check_vma=False)
```

```python
import math

import jax
import jax.numpy as jnp
from jax import lax
from jax.experimental import pallas as pl
from jax.experimental.pallas import tpu as pltpu
from jax.sharding import PartitionSpec as P

f32 = jnp.float32
bf16 = jnp.bfloat16
NEG = -1e30
LOG2E = 1.4426950408889634
MESH = pl.DeviceIdType.MESH

NZ, NX, NY = 8, 4, 4
BLK = 128
PACK = 144
LAT = 512
NEW_ROWS = 64
CH = 4 * BLK
HALF = 512
ROWS = 2 * HALF

NEAR = (0, 1, 7, 2)
FAR = (6, 3, 5, 4)
SPOT = {d: n for n, d in enumerate(NEAR + FAR)}

ORDER = [
    (0, 0, 0), (1, 0, 0), (0, 1, 0), (0, 2, 0),
    (0, 0, 1), (0, 0, 2), (1, 1, 0), (1, 2, 0),
    (1, 0, 1), (1, 0, 2), (0, 3, 0), (0, 0, 3),
    (0, 1, 1), (0, 1, 2), (0, 2, 1), (0, 2, 2),
    (1, 3, 0), (1, 0, 3), (1, 1, 1), (1, 1, 2),
    (1, 2, 1), (1, 2, 2), (0, 3, 1), (0, 3, 2),
    (0, 1, 3), (0, 2, 3), (1, 3, 1), (1, 3, 2),
    (1, 1, 3), (1, 2, 3), (0, 3, 3), (1, 3, 3),
]
PLACE = {b: n for n, b in enumerate(ORDER)}
OFFSET = (0, 3, 1, 2)

N, F = 0, 1
UNITS = [
    (N, 0), (N, 1), (F, 0), (F, 1), (N, 2), (F, 2), (F, 3), (F, 4),
    (F, 5), (F, 6), (F, 7), (N, 3), (N, 4), (N, 5), (N, 6), (N, 7),
]
PASS = {
    0: [(1, 0), (2, 0), (0, 1), (0, 2)],
    2: [(3, 0), (0, 3)],
    3: [(1, 1), (1, 2)],
    4: [(2, 1), (2, 2)],
    5: [(3, 1)],
    6: [(3, 2), (1, 3)],
    7: [(2, 3)],
    8: [(3, 3)],
}


def dot_t(a, b):
    return lax.dot_general(a, b, (((1,), (1,)), ((), ())), preferred_element_type=f32)


def dot_n(a, b):
    return jnp.dot(a, b, preferred_element_type=f32)


def kernel(
    scale, q_hbm, cache_hbm, new_hbm, len_ref, wk_hbm, wv_hbm, out_ref,
    q_ref, cache_ref, new_ref, kbuf, ktail, nsend, nbuf, qsend, qrecv, qabs, qn, wk, wv, sa, sb, pa, pb, al, top, tot, acc, ob, osend, orecv, ssend, srecv,
    w_sem, send_sem, k_sem, s_sem, q_sem, n_sem, o_sem, t_sem,
):
    ctx = lax.axis_index("ctx")
    head = lax.axis_index("head")
    z, x = ctx // NX, ctx % NX
    y, c = head // 2, head % 2

    def at(zz, xx, yy, cc):
        return (zz * NX + xx, yy * 2 + cc)

    on_x, on_y = 1 - c, c
    ax1p = at(z, (x + on_x) % NX, (y + on_y) % NY, c)
    ax1m = at(z, (x + 3 * on_x) % NX, (y + 3 * on_y) % NY, c)
    ax2p = at(z, (x + on_y) % NX, (y + on_x) % NY, c)
    ax2m = at(z, (x + 3 * on_y) % NX, (y + 3 * on_x) % NY, c)
    sib = at(z, x, y, 1 - c)
    z_to = [None] + [at((z + d) % NZ, x, y, c) for d in range(1, NZ)]
    x_to = [None] + [at(z, (x + d) % NX, y, c) for d in range(1, NX)]

    barrier = pltpu.get_barrier_semaphore()
    partners = [ax1p, ax1m, ax2p, ax2m, sib] + z_to[1:] + x_to[1:]
    for who in partners:
        pl.semaphore_signal(barrier, inc=1, device_id=who, device_id_type=MESH)
    pairs = [(cache_hbm, cache_ref), (q_hbm, q_ref), (new_hbm, new_ref), (wk_hbm, wk), (wv_hbm, wv)]
    loads = [pltpu.make_async_copy(src, dst, w_sem.at[n]) for n, (src, dst) in enumerate(pairs)]
    for load in loads:
        load.start()
    wk_copy, wv_copy = loads[3:]
    for load in loads[:3]:
        load.wait()

    length = len_ref[0]
    mine = kbuf.at[0]
    qsend[0:128, :] = q_ref[:, 0:128]
    qsend[128:192, :] = jnp.concatenate([q_ref[0:64, 128:192], q_ref[64:128, 128:192]], axis=1)
    for n in range(4):
        mine[0:128, 128 * n : 128 * n + 128] = cache_ref[128 * n : 128 * n + 128, :].astype(f32).T.astype(bf16)
    rope = jnp.concatenate([cache_ref[LAT:576, :].astype(f32), jnp.zeros((64, 128), f32)], axis=0).T
    mine[128:144, :] = jnp.concatenate([rope[16 * g : 16 * g + 16, 0:64] for g in range(8)], axis=1).astype(bf16)
    fresh = new_ref[...].astype(f32)
    fresh = jnp.concatenate([fresh, jnp.zeros((8, 576), f32)], axis=0)
    fresh = jnp.concatenate([fresh, jnp.zeros((16, 64), f32)], axis=1).astype(bf16)
    nbuf[0] = fresh
    nsend[...] = fresh

    pl.semaphore_wait(barrier, len(partners))

    def send(kind, src, dst, who, recv):
        pltpu.make_async_remote_copy(
            src_ref=src, dst_ref=dst, send_sem=send_sem.at[kind], recv_sem=recv, device_id=who, device_id_type=MESH
        ).start()

    def rows_of(block, half=None):
        ref = kbuf.at[PLACE[block]]
        return ref if half is None else ref.at[0:80] if half == 0 else ref.at[80:144]

    def k_send(block, to_block, who, half=None):
        _, d1, d2 = to_block
        send(0, rows_of(block, half), rows_of(to_block, half), who, k_sem.at[d1 * 4 + d2])

    def sib_send(d1, d2):
        block = (1, d1, d2)
        send(0, rows_of((0, d1, d2)), rows_of(block), sib, s_sem.at[PLACE[block] // 4])

    def wait_at(ref, sem):
        pltpu.make_async_copy(ref, ref, sem).wait()

    def wait_sib(chunk):
        count = sum(b[0] for b in ORDER[4 * chunk : 4 * chunk + 4])
        if count:
            wait_at(kbuf.at[4 * chunk : 4 * chunk + count], s_sem.at[chunk])

    def event(d1, d2):
        block = (0, d1, d2)
        wait_at(rows_of(block), k_sem.at[d1 * 4 + d2])
        if d2 == 0:
            if d1 == 1:
                k_send(block, (0, 3, 0), ax1p, 0)
            if d1 == 2:
                k_send(block, (0, 3, 0), ax1m, 1)
            k_send(block, (0, d1, 1), ax2p)
            k_send(block, (0, d1, 2), ax2m)
        elif d2 == 1:
            k_send(block, (0, d1, 3), ax2p, 0)
        elif d2 == 2:
            k_send(block, (0, d1, 3), ax2m, 1)
        sib_send(d1, d2)

    def q_send(d, to, half=None, src=None):
        part = slice(0, 192) if half is None else slice(96 * half, 96 * half + 96)
        src = qsend if src is None else src
        send(1, src.at[part], qrecv.at[d, part], to, q_sem.at[d])

    q_send(1, z_to[1])
    q_send(7, z_to[7])
    q_send(2, z_to[2])
    q_send(6, z_to[6])
    own = (0, 0, 0)
    k_send(own, (0, 1, 0), ax1p)
    k_send(own, (0, 2, 0), ax1m)
    k_send(own, (0, 0, 1), ax2p)
    k_send(own, (0, 0, 2), ax2m)
    sib_send(0, 0)
    for d in range(1, NX):
        send(2, nsend, nbuf.at[d], x_to[d], n_sem.at[0])

    def place(d):
        r = slice(128 * SPOT[d], 128 * SPOT[d] + 128)
        lane64 = lax.broadcasted_iota(jnp.int32, (128, 64), 1)
        row_j = lax.broadcasted_iota(jnp.int32, (128, 64), 0) // 16
        block = qsend if d == 0 else qrecv.at[d]
        qn[r, :] = block[0:128, :].astype(f32)
        rope = block[128:192, :]
        rope = jnp.concatenate([rope[:, 0:64], rope[:, 64:128]], axis=0)
        pick = jnp.where(lane64 == d * 8 + row_j, 1.0, 0.0).astype(bf16)
        qabs[r, LAT:640] = jnp.concatenate([rope, pick], axis=1)

    def absorb(half):
        for h in range(16):
            part = qn[pl.ds(HALF * half + h, 32, stride=16), :].astype(bf16)
            lat = dot_n(part, wk[h])
            for n in range(4):
                acc[n, pl.ds(HALF * half + h, 32, stride=16), :] = lat[:, 128 * n : 128 * n + 128]
        for t in range(8):
            r = slice(HALF * half + 64 * t, HALF * half + 64 * t + 64)
            for n in range(4):
                qabs[r, 128 * n : 128 * n + 128] = acc[n, r, :].astype(bf16)

    def unpack(block):
        plane, d1, d2 = block
        first_x = on_x if plane == 0 else on_y
        s1, s2 = OFFSET[d1], OFFSET[d2]
        sx = (x + s1 * first_x + s2 * (1 - first_x)) % NX
        sy = (y + s1 * (1 - first_x) + s2 * first_x) % NY
        sc = c if plane == 0 else 1 - c
        slot = ((z * NX + sx) * NY + sy) * (2 * BLK) + sc * BLK
        here = PLACE[block]
        packed = kbuf[here, 128:144, :].astype(f32)
        row = lax.broadcasted_iota(jnp.int32, (16, 128), 0)
        lane = lax.broadcasted_iota(jnp.int32, (16, 128), 1)
        for g in range(8):
            piece = packed[:, 128 * (g // 2) : 128 * (g // 2) + 128]
            if g % 2:
                piece = pltpu.roll(piece, 64, 1)
            bias = jnp.where(slot + 16 * g + row < length, 0.0, NEG)
            ktail[BLK * here + 16 * g : BLK * here + 16 * g + 16, :] = jnp.where(lane < 64, piece, bias).astype(bf16)

    def mask_new():
        wait_at(nbuf.at[1:NX], n_sem.at[0])
        n_j = lax.broadcasted_iota(jnp.int32, (16, 128), 0)
        col = lax.broadcasted_iota(jnp.int32, (16, 128), 1) - 64
        q_rank = (col % 8) * (NZ * NX) + (z + NZ - col // 8) % NZ * NX + x
        for d in range(NX):
            n_rank = n_j * (NZ * NX) + z * NX + (x + NX - d) % NX
            bias = jnp.where((n_j < 8) & (n_rank <= q_rank), 0.0, NEG)
            tail = nbuf[d, :, LAT:640].astype(f32)
            nbuf[d, :, LAT:640] = jnp.where(col >= 0, bias, tail).astype(bf16)

    def keys_of(chunk, lo):
        if lo == CH:
            return jnp.concatenate([nbuf[d] for d in range(NX)], axis=0)
        b = chunk * 4 + lo // BLK
        lat = jnp.concatenate([kbuf[b, 0:128, :], kbuf[b + 1, 0:128, :]], axis=0)
        return jnp.concatenate([lat, ktail[BLK * b : BLK * b + 256, :]], axis=1)

    def scores(unit, s):
        half, chunk = unit
        q = qabs.at[HALF * half : HALF * half + HALF]
        for lo in range(0, CH, 256):
            s[:, lo : lo + 256] = dot_t(q[...], keys_of(chunk, lo))
        if chunk == 0:
            s[:, CH : CH + NEW_ROWS] = dot_t(q[...], keys_of(chunk, CH))

    def weigh(unit, s, p):
        half, chunk = unit
        size = CH + NEW_ROWS if chunk == 0 else CH
        for t in range(HALF // 32):
            sr = slice(32 * t, 32 * t + 32)
            r = slice(HALF * half + 32 * t, HALF * half + 32 * t + 32)
            sc = s[sr, 0:size]
            new_top = jnp.broadcast_to(jnp.max(sc, axis=1, keepdims=True), (32, 128))
            if chunk:
                old_top = top[r, :]
                new_top = jnp.maximum(old_top, new_top)
                shrink = jnp.exp2((old_top - new_top) * scale)
                al[sr, :] = shrink
            top[r, :] = new_top
            w = jnp.exp2((sc - new_top[:, 0:1]) * scale)
            part = w[:, 0:128]
            for lo in range(128, CH, 128):
                part = part + w[:, lo : lo + 128]
            if size > CH:
                part = part + jnp.concatenate([w[:, CH:size], jnp.zeros((32, 128 - NEW_ROWS), f32)], axis=1)
            if chunk:
                part = part + tot[r, :] * shrink
            tot[r, :] = part
            p[sr, 0:size] = w.astype(bf16)

    def mix(unit, p):
        half, chunk = unit
        size = CH + NEW_ROWS if chunk == 0 else CH
        for n in range(2):
            cols = slice(256 * n, 256 * n + 256)
            v = [kbuf[chunk * 4 + b, 0:128, cols] for b in range(4)]
            if chunk == 0:
                v = v + [nbuf[d, :, cols] for d in range(NX)]
            v = jnp.concatenate(v, axis=0)
            for t in range(HALF // 256):
                sr = slice(256 * t, 256 * t + 256)
                r = slice(HALF * half + 256 * t, HALF * half + 256 * t + 256)
                o = dot_n(p[sr, 0:size], v)
                for k in range(2):
                    part = o[:, 128 * k : 128 * k + 128]
                    m = 2 * n + k
                    acc[m, r, :] = part if chunk == 0 else acc[m, r, :] * al[sr, :] + part

    def deliver(half):
        lane = lax.broadcasted_iota(jnp.int32, (128, 128), 1)
        owners = NEAR if half == N else FAR
        for d in owners:
            r = slice(128 * SPOT[d], 128 * SPOT[d] + 128)
            total = jnp.sum(tot[r, :], axis=1, keepdims=True)
            ssend[d] = jnp.where(lane == 0, top[r, :], total).T[0:8, :]
            if d:
                send(3, ssend.at[d], srecv.at[d], z_to[NZ - d], t_sem.at[0])
        for h in range(16):
            rows = pl.ds(HALF * half + h, 32, stride=16)
            part = jnp.concatenate([acc[n, rows, :] for n in range(4)], axis=1)
            hi = part.astype(bf16)
            lo = (part - hi.astype(f32)).astype(bf16)
            both = dot_n(jnp.concatenate([hi, lo], axis=0), wv[h])
            ob[rows, :] = both[0:32] + both[32:64]
        for d in owners:
            if d:
                osend[d] = ob[128 * SPOT[d] : 128 * SPOT[d] + 128, :].astype(bf16)
                send(4, osend.at[d], orecv.at[d], z_to[NZ - d], o_sem.at[half])

    def relay():
        wait_at(qrecv.at[2], q_sem.at[2])
        q_send(3, z_to[1], src=qrecv.at[2])
        q_send(4, z_to[2], half=0, src=qrecv.at[2])
        wait_at(qrecv.at[6], q_sem.at[6])
        q_send(5, z_to[7], src=qrecv.at[6])
        q_send(4, z_to[6], half=1, src=qrecv.at[6])

    def take_near():
        wait_at(qrecv.at[1], q_sem.at[1])
        wait_at(qrecv.at[7], q_sem.at[7])
        for d in NEAR:
            place(d)

    def take_far():
        wait_at(qrecv.at[3], q_sem.at[3])
        wait_at(qrecv.at[5], q_sem.at[5])
        wait_at(qrecv.at[4], q_sem.at[4])
        for d in FAR:
            place(d)

    ready = set()
    sib_in = set()

    def before(n):
        half, chunk = UNITS[n]
        if n == 0:
            relay()
        for b in PASS.get(n, ()):
            event(*b)
        if n == 0:
            take_near()
            wk_copy.wait()
            absorb(N)
        if (half, chunk) == (F, 0):
            take_far()
            absorb(F)
        if n == 0:
            mask_new()
        if chunk in ready:
            return
        ready.add(chunk)
        wait_sib(chunk)
        for b in ORDER[4 * chunk : 4 * chunk + 4]:
            unpack(b)

    before(0)
    scores(UNITS[0], sa)
    for n, unit in enumerate(UNITS):
        s_now, s_next, p = (sa, sb, pa) if n % 2 == 0 else (sb, sa, pb)
        if n + 1 < len(UNITS):
            before(n + 1)
            scores(UNITS[n + 1], s_next)
        weigh(unit, s_now, p)
        mix(unit, p)
        if unit == (F, 7):
            wv_copy.wait()
            deliver(F)
    deliver(N)

    wait_at(srecv.at[1:NZ], t_sem.at[0])
    tops = [ssend[0, 0:1, :]] + [srecv[d, 0:1, :] for d in range(1, NZ)]
    totals = [ssend[0, 1:2, :]] + [srecv[d, 1:2, :] for d in range(1, NZ)]
    best = tops[0]
    for d in range(1, NZ):
        best = jnp.maximum(best, tops[d])
    shares = [jnp.exp2((t - best) * scale) for t in tops]
    full = shares[0] * totals[0]
    for d in range(1, NZ):
        full = full + shares[d] * totals[d]
    shares = [s / full for s in shares]
    by_row = jnp.concatenate(shares + [jnp.zeros((120, 128), f32)], axis=0).T
    result = ob[0:128, :] * by_row[:, 0:1]
    wait_at(orecv.at[0:4], o_sem.at[F])
    for d in FAR + NEAR[1:]:
        if d == NEAR[1]:
            wait_at(orecv.at[0:3], o_sem.at[N])
        result = result + orecv[d].astype(f32) * by_row[:, d : d + 1]
    out_ref[...] = result.astype(bf16)
    for kind, ref in enumerate((kbuf.at[0:31], qrecv.at[0:7], nbuf.at[0:3], ssend.at[0:7], osend.at[0:7])):
        wait_at(ref, send_sem.at[kind])


def body(queries, absorb_k, absorb_v, cache, new_entries, cache_len):
    scale = LOG2E / math.sqrt(queries.shape[2])
    vmem = pl.BlockSpec(memory_space=pltpu.VMEM)
    hbm = pl.BlockSpec(memory_space=pl.ANY)
    dma = pltpu.SemaphoreType.DMA

    def run(*refs):
        kernel(scale, *refs)

    out = pl.pallas_call(
        run,
        out_shape=jax.ShapeDtypeStruct((128, 128), bf16),
        in_specs=[hbm, hbm, hbm, pl.BlockSpec(memory_space=pltpu.SMEM), hbm, hbm],
        out_specs=vmem,
        scratch_shapes=[
            pltpu.VMEM((128, 192), bf16),
            pltpu.VMEM((576, 128), bf16),
            pltpu.VMEM((8, 576), bf16),
            pltpu.VMEM((32, PACK, LAT), bf16),
            pltpu.VMEM((32 * BLK, 128), bf16),
            pltpu.VMEM((16, 640), bf16),
            pltpu.VMEM((NX, 16, 640), bf16),
            pltpu.VMEM((192, 128), bf16),
            pltpu.VMEM((NZ, 192, 128), bf16),
            pltpu.VMEM((ROWS, 640), bf16),
            pltpu.VMEM((ROWS, 128), f32),
            pltpu.VMEM((16, 128, LAT), bf16),
            pltpu.VMEM((16, LAT, 128), bf16),
            pltpu.VMEM((HALF, 640), f32),
            pltpu.VMEM((HALF, 640), f32),
            pltpu.VMEM((HALF, 640), bf16),
            pltpu.VMEM((HALF, 640), bf16),
            pltpu.VMEM((HALF, 128), f32),
            pltpu.VMEM((ROWS, 128), f32),
            pltpu.VMEM((ROWS, 128), f32),
            pltpu.VMEM((4, ROWS, 128), f32),
            pltpu.VMEM((ROWS, 128), f32),
            pltpu.VMEM((NZ, 128, 128), bf16),
            pltpu.VMEM((NZ, 128, 128), bf16),
            pltpu.VMEM((NZ, 8, 128), f32),
            pltpu.VMEM((NZ, 8, 128), f32),
            dma((5,)),
            dma((5,)),
            dma((16,)),
            dma((8,)),
            dma((NZ,)),
            dma((1,)),
            dma((2,)),
            dma((1,)),
        ],
        compiler_params=pltpu.CompilerParams(
            collective_id=0, has_side_effects=True, vmem_limit_bytes=56 << 20
        ),
    )(queries.reshape(128, 192), cache.T, new_entries, cache_len, absorb_k, absorb_v)
    return out.reshape(8, 16, 128)


def solution(mesh):
    in_specs = (
        P("ctx", "head", None),
        P("head", None, None),
        P("head", None, None),
        P(("ctx", "head"), None),
        P("ctx", None),
        P(),
    )
    out_specs = P("ctx", "head", None)
    return jax.shard_map(body, mesh=mesh, in_specs=in_specs, out_specs=out_specs, check_vma=False)
```

```python
import math

import jax
import jax.numpy as jnp
from jax import lax
from jax.experimental import pallas as pl
from jax.experimental.pallas import tpu as pltpu
from jax.sharding import PartitionSpec as P

f32 = jnp.float32
bf16 = jnp.bfloat16
NEG = -1e30
LOG2E = 1.4426950408889634
MESH = pl.DeviceIdType.MESH

NZ, NX, NY = 8, 4, 4
BLK = 128
WIDE = 576
MASK = 64
LAT = 512
NEW_ROWS = 64
CH = 4 * BLK
HALF = 512
ROWS = 2 * HALF

NEAR = (0, 1, 7, 2)
FAR = (6, 3, 5, 4)
SPOT = {d: n for n, d in enumerate(NEAR + FAR)}

ORDER = [
    (0, 0, 0), (1, 0, 0), (0, 1, 0), (0, 2, 0),
    (0, 0, 1), (0, 0, 2), (1, 1, 0), (1, 2, 0),
    (1, 0, 1), (1, 0, 2), (0, 3, 0), (0, 0, 3),
    (0, 1, 1), (0, 1, 2), (0, 2, 1), (0, 2, 2),
    (1, 3, 0), (1, 0, 3), (1, 1, 1), (1, 1, 2),
    (1, 2, 1), (1, 2, 2), (0, 3, 1), (0, 3, 2),
    (0, 1, 3), (0, 2, 3), (1, 3, 1), (1, 3, 2),
    (1, 1, 3), (1, 2, 3), (0, 3, 3), (1, 3, 3),
]
PLACE = {b: n for n, b in enumerate(ORDER)}
OFFSET = (0, 3, 1, 2)

N, F = 0, 1
UNITS = [
    (N, 0), (N, 1), (F, 0), (F, 1), (N, 2), (F, 2), (F, 3), (F, 4),
    (F, 5), (F, 6), (F, 7), (N, 3), (N, 4), (N, 5), (N, 6), (N, 7),
]
PASS = {
    0: [(1, 0), (2, 0), (0, 1), (0, 2)],
    2: [(3, 0), (0, 3)],
    3: [(1, 1), (1, 2)],
    4: [(2, 1), (2, 2)],
    5: [(3, 1)],
    6: [(3, 2), (1, 3)],
    7: [(2, 3)],
    8: [(3, 3)],
}


def dot_t(a, b):
    return lax.dot_general(a, b, (((1,), (1,)), ((), ())), preferred_element_type=f32)


def dot_n(a, b):
    return jnp.dot(a, b, preferred_element_type=f32)


def kernel(
    scale, q_hbm, cache_hbm, new_hbm, len_ref, wk_hbm, wv_hbm, out_ref,
    q_ref, new_ref, kbuf, kbias, nsend, nbuf, newk, qsend, qrecv, qabs, qn, wk, wv, sa, sb, pa, pb, al, top, tot, acc, ob, osend, orecv, ssend, srecv,
    w_sem, send_sem, k_sem, s_sem, q_sem, n_sem, o_sem, t_sem,
):
    ctx = lax.axis_index("ctx")
    head = lax.axis_index("head")
    z, x = ctx // NX, ctx % NX
    y, c = head // 2, head % 2

    def at(zz, xx, yy, cc):
        return (zz * NX + xx, yy * 2 + cc)

    on_x, on_y = 1 - c, c
    ax1p = at(z, (x + on_x) % NX, (y + on_y) % NY, c)
    ax1m = at(z, (x + 3 * on_x) % NX, (y + 3 * on_y) % NY, c)
    ax2p = at(z, (x + on_y) % NX, (y + on_x) % NY, c)
    ax2m = at(z, (x + 3 * on_y) % NX, (y + 3 * on_x) % NY, c)
    sib = at(z, x, y, 1 - c)
    z_to = [None] + [at((z + d) % NZ, x, y, c) for d in range(1, NZ)]
    x_to = [None] + [at(z, (x + d) % NX, y, c) for d in range(1, NX)]

    barrier = pltpu.get_barrier_semaphore()
    partners = [ax1p, ax1m, ax2p, ax2m, sib] + z_to[1:] + x_to[1:]
    for who in partners:
        pl.semaphore_signal(barrier, inc=1, device_id=who, device_id_type=MESH)
    pairs = [(q_hbm, q_ref), (new_hbm, new_ref), (cache_hbm, kbuf.at[0]), (wk_hbm, wk), (wv_hbm, wv)]
    loads = [pltpu.make_async_copy(src, dst, w_sem.at[n]) for n, (src, dst) in enumerate(pairs)]
    for load in loads:
        load.start()
    own_copy, wk_copy, wv_copy = loads[2:]
    for load in loads[:2]:
        load.wait()

    length = len_ref[0]
    qsend[0:128, :] = q_ref[:, 0:128]
    qsend[128:192, :] = jnp.concatenate([q_ref[0:64, 128:192], q_ref[64:128, 128:192]], axis=1)
    fresh = new_ref[...].astype(f32)
    fresh = jnp.concatenate([fresh, jnp.zeros((8, 576), f32)], axis=0)
    fresh = jnp.concatenate([fresh, jnp.zeros((16, 64), f32)], axis=1).astype(bf16)
    nbuf[0] = fresh
    nsend[...] = fresh

    pl.semaphore_wait(barrier, len(partners))

    def send(kind, src, dst, who, recv):
        pltpu.make_async_remote_copy(
            src_ref=src, dst_ref=dst, send_sem=send_sem.at[kind], recv_sem=recv, device_id=who, device_id_type=MESH
        ).start()

    def rows_of(block, half=None):
        ref = kbuf.at[PLACE[block]]
        return ref if half is None else ref.at[288 * half : 288 * half + 288]

    def k_send(block, to_block, who, half):
        _, d1, d2 = to_block
        src = cache_hbm.at[288 * half : 288 * half + 288] if block == (0, 0, 0) else rows_of(block, half)
        send(0, src, rows_of(to_block, half), who, k_sem.at[d1 * 4 + d2, half])

    def sib_send(d1, d2):
        block = (1, d1, d2)
        src = rows_of((0, d1, d2)) if d1 or d2 else cache_hbm
        send(0, src, rows_of(block), sib, s_sem.at[PLACE[block] // 4])

    def wait_at(ref, sem):
        pltpu.make_async_copy(ref, ref, sem).wait()

    def wait_sib(chunk):
        count = sum(b[0] for b in ORDER[4 * chunk : 4 * chunk + 4])
        if count:
            wait_at(kbuf.at[4 * chunk : 4 * chunk + count], s_sem.at[chunk])

    def half_event(d1, d2, half):
        block = (0, d1, d2)
        wait_at(rows_of(block, half), k_sem.at[d1 * 4 + d2, half])
        if d2 == 0:
            if d1 == 1 and half == 0:
                k_send(block, (0, 3, 0), ax1p, 0)
            if d1 == 2 and half == 1:
                k_send(block, (0, 3, 0), ax1m, 1)
            k_send(block, (0, d1, 1), ax2p, half)
            k_send(block, (0, d1, 2), ax2m, half)
        elif d2 == 1 and half == 0:
            k_send(block, (0, d1, 3), ax2p, 0)
        elif d2 == 2 and half == 1:
            k_send(block, (0, d1, 3), ax2m, 1)

    def event(*blocks):
        for turn in range(2):
            for d1, d2 in blocks:
                first = 1 if (d2 or d1) == 2 else 0
                half_event(d1, d2, first ^ turn)
        for d1, d2 in blocks:
            sib_send(d1, d2)

    def q_send(d, to, half=None, src=None):
        part = slice(0, 192) if half is None else slice(96 * half, 96 * half + 96)
        src = qsend if src is None else src
        send(1, src.at[part], qrecv.at[d, part], to, q_sem.at[d])

    q_send(1, z_to[1])
    q_send(7, z_to[7])
    q_send(2, z_to[2])
    q_send(6, z_to[6])
    own = (0, 0, 0)
    for turn in range(2):
        k_send(own, (0, 1, 0), ax1p, turn)
        k_send(own, (0, 2, 0), ax1m, 1 - turn)
    for turn in range(2):
        k_send(own, (0, 0, 1), ax2p, turn)
        k_send(own, (0, 0, 2), ax2m, 1 - turn)
    sib_send(0, 0)
    for d in range(1, NX):
        send(2, nsend, nbuf.at[d], x_to[d], n_sem.at[0])

    def place(d):
        r = slice(128 * SPOT[d], 128 * SPOT[d] + 128)
        lane64 = lax.broadcasted_iota(jnp.int32, (128, 64), 1)
        row_j = lax.broadcasted_iota(jnp.int32, (128, 64), 0) // 16
        block = qsend if d == 0 else qrecv.at[d]
        qn[r, :] = block[0:128, :].astype(f32)
        rope = block[128:192, :]
        rope = jnp.concatenate([rope[:, 0:64], rope[:, 64:128]], axis=0)
        pick = jnp.where(lane64 == d * 8 + row_j, 1.0, 0.0).astype(bf16)
        qabs[r, LAT:640] = jnp.concatenate([rope, pick], axis=1)

    def absorb(half):
        for h in range(16):
            part = qn[pl.ds(HALF * half + h, 32, stride=16), :].astype(bf16)
            lat = dot_n(part, wk[h])
            for n in range(4):
                acc[n, pl.ds(HALF * half + h, 32, stride=16), :] = lat[:, 128 * n : 128 * n + 128]
        for t in range(8):
            r = slice(HALF * half + 64 * t, HALF * half + 64 * t + 64)
            for n in range(4):
                qabs[r, 128 * n : 128 * n + 128] = acc[n, r, :].astype(bf16)

    def mask_slots(block):
        plane, d1, d2 = block
        first_x = on_x if plane == 0 else on_y
        s1, s2 = OFFSET[d1], OFFSET[d2]
        sx = (x + s1 * first_x + s2 * (1 - first_x)) % NX
        sy = (y + s1 * (1 - first_x) + s2 * first_x) % NY
        sc = c if plane == 0 else 1 - c
        slot = ((z * NX + sx) * NY + sy) * (2 * BLK) + sc * BLK
        here = PLACE[block] * BLK
        key = lax.broadcasted_iota(jnp.int32, (MASK, BLK), 1)
        kbias[:, here : here + BLK] = jnp.where(slot + key < length, 0.0, NEG).astype(bf16)

    def take_new():
        wait_at(nbuf.at[1:NX], n_sem.at[0])
        rows = [nbuf[d].astype(f32) for d in range(NX)] + [jnp.zeros((NEW_ROWS, 640), f32)]
        rows = jnp.concatenate(rows, axis=0)
        for n in range(5):
            newk[128 * n : 128 * n + 128, :] = rows[:, 128 * n : 128 * n + 128].T.astype(bf16)
        key = lax.broadcasted_iota(jnp.int32, (MASK, BLK), 1)
        row = lax.broadcasted_iota(jnp.int32, (MASK, BLK), 0)
        n_j = key % 16
        n_rank = n_j * (NZ * NX) + z * NX + (x + NX - key // 16) % NX
        q_rank = (row % 8) * (NZ * NX) + (z + NZ - row // 8) % NZ * NX + x
        seen = (key < NEW_ROWS) & (n_j < 8) & (n_rank <= q_rank)
        newk[WIDE : WIDE + MASK, :] = jnp.where(seen, 0.0, NEG).astype(bf16)

    def keys_of(b):
        both = jnp.concatenate([kbuf[b], kbuf[b + 1]], axis=1)
        return jnp.concatenate([both, kbias[:, BLK * b : BLK * b + 2 * BLK]], axis=0)

    def scores(unit, s):
        half, chunk = unit
        q = qabs.at[HALF * half : HALF * half + HALF]
        for lo in range(0, CH, 256):
            s[:, lo : lo + 256] = dot_n(q[...], keys_of(4 * chunk + lo // BLK))
        if chunk == 0:
            s[:, CH : CH + BLK] = dot_n(q[...], newk[...])

    def weigh(unit, s, p):
        half, chunk = unit
        size = CH + BLK if chunk == 0 else CH
        for t in range(HALF // 32):
            sr = slice(32 * t, 32 * t + 32)
            r = slice(HALF * half + 32 * t, HALF * half + 32 * t + 32)
            sc = s[sr, 0:size]
            new_top = jnp.broadcast_to(jnp.max(sc, axis=1, keepdims=True), (32, 128))
            if chunk:
                old_top = top[r, :]
                new_top = jnp.maximum(old_top, new_top)
                shrink = jnp.exp2((old_top - new_top) * scale)
                al[sr, :] = shrink
            top[r, :] = new_top
            w = jnp.exp2((sc - new_top[:, 0:1]) * scale)
            part = w[:, 0:128]
            for lo in range(128, size, 128):
                part = part + w[:, lo : lo + 128]
            if chunk:
                part = part + tot[r, :] * shrink
            tot[r, :] = part
            p[sr, 0:size] = w.astype(bf16)

    def mix(unit, p):
        half, chunk = unit
        size = CH + BLK if chunk == 0 else CH
        for n in range(2):
            cols = slice(256 * n, 256 * n + 256)
            v = [kbuf[chunk * 4 + b, cols, :] for b in range(4)]
            if chunk == 0:
                v = v + [newk[cols, :]]
            v = jnp.concatenate(v, axis=1)
            for t in range(HALF // 256):
                sr = slice(256 * t, 256 * t + 256)
                r = slice(HALF * half + 256 * t, HALF * half + 256 * t + 256)
                o = dot_t(p[sr, 0:size], v)
                for k in range(2):
                    part = o[:, 128 * k : 128 * k + 128]
                    m = 2 * n + k
                    acc[m, r, :] = part if chunk == 0 else acc[m, r, :] * al[sr, :] + part

    def deliver(half):
        lane = lax.broadcasted_iota(jnp.int32, (128, 128), 1)
        owners = NEAR if half == N else FAR
        for d in owners:
            r = slice(128 * SPOT[d], 128 * SPOT[d] + 128)
            total = jnp.sum(tot[r, :], axis=1, keepdims=True)
            ssend[d] = jnp.where(lane == 0, top[r, :], total).T[0:8, :]
            if d:
                send(3, ssend.at[d], srecv.at[d], z_to[NZ - d], t_sem.at[0])
        for h in range(16):
            rows = pl.ds(HALF * half + h, 32, stride=16)
            part = jnp.concatenate([acc[n, rows, :] for n in range(4)], axis=1)
            hi = part.astype(bf16)
            lo = (part - hi.astype(f32)).astype(bf16)
            both = dot_n(jnp.concatenate([hi, lo], axis=0), wv[h])
            ob[rows, :] = both[0:32] + both[32:64]
        for d in owners:
            if d:
                osend[d] = ob[128 * SPOT[d] : 128 * SPOT[d] + 128, :].astype(bf16)
                send(4, osend.at[d], orecv.at[d], z_to[NZ - d], o_sem.at[half])

    def relay():
        wait_at(qrecv.at[2], q_sem.at[2])
        q_send(3, z_to[1], src=qrecv.at[2])
        q_send(4, z_to[2], half=0, src=qrecv.at[2])
        wait_at(qrecv.at[6], q_sem.at[6])
        q_send(5, z_to[7], src=qrecv.at[6])
        q_send(4, z_to[6], half=1, src=qrecv.at[6])

    def take_near():
        wait_at(qrecv.at[1], q_sem.at[1])
        wait_at(qrecv.at[7], q_sem.at[7])
        for d in NEAR:
            place(d)

    def take_far():
        wait_at(qrecv.at[3], q_sem.at[3])
        wait_at(qrecv.at[5], q_sem.at[5])
        wait_at(qrecv.at[4], q_sem.at[4])
        for d in FAR:
            place(d)

    ready = set()
    sib_in = set()

    def before(n):
        half, chunk = UNITS[n]
        if n == 0:
            relay()
        event(*PASS.get(n, ()))
        if n == 0:
            take_near()
            wk_copy.wait()
            absorb(N)
        if (half, chunk) == (F, 0):
            take_far()
            absorb(F)
        if n == 0:
            take_new()
            own_copy.wait()
        if chunk in ready:
            return
        ready.add(chunk)
        wait_sib(chunk)
        for b in ORDER[4 * chunk : 4 * chunk + 4]:
            mask_slots(b)

    before(0)
    scores(UNITS[0], sa)
    for n, unit in enumerate(UNITS):
        s_now, s_next, p = (sa, sb, pa) if n % 2 == 0 else (sb, sa, pb)
        if n + 1 < len(UNITS):
            before(n + 1)
            scores(UNITS[n + 1], s_next)
        weigh(unit, s_now, p)
        mix(unit, p)
        if unit == (F, 7):
            wv_copy.wait()
            deliver(F)
    deliver(N)

    wait_at(srecv.at[1:NZ], t_sem.at[0])
    tops = [ssend[0, 0:1, :]] + [srecv[d, 0:1, :] for d in range(1, NZ)]
    totals = [ssend[0, 1:2, :]] + [srecv[d, 1:2, :] for d in range(1, NZ)]
    best = tops[0]
    for d in range(1, NZ):
        best = jnp.maximum(best, tops[d])
    shares = [jnp.exp2((t - best) * scale) for t in tops]
    full = shares[0] * totals[0]
    for d in range(1, NZ):
        full = full + shares[d] * totals[d]
    shares = [s / full for s in shares]
    by_row = jnp.concatenate(shares + [jnp.zeros((120, 128), f32)], axis=0).T
    result = ob[0:128, :] * by_row[:, 0:1]
    wait_at(orecv.at[0:4], o_sem.at[F])
    for d in FAR + NEAR[1:]:
        if d == NEAR[1]:
            wait_at(orecv.at[0:3], o_sem.at[N])
        result = result + orecv[d].astype(f32) * by_row[:, d : d + 1]
    out_ref[...] = result.astype(bf16)
    for kind, ref in enumerate((kbuf.at[0:31], qrecv.at[0:7], nbuf.at[0:3], ssend.at[0:7], osend.at[0:7])):
        wait_at(ref, send_sem.at[kind])


def body(queries, absorb_k, absorb_v, cache, new_entries, cache_len):
    scale = LOG2E / math.sqrt(queries.shape[2])
    vmem = pl.BlockSpec(memory_space=pltpu.VMEM)
    hbm = pl.BlockSpec(memory_space=pl.ANY)
    dma = pltpu.SemaphoreType.DMA

    def run(*refs):
        kernel(scale, *refs)

    out = pl.pallas_call(
        run,
        out_shape=jax.ShapeDtypeStruct((128, 128), bf16),
        in_specs=[hbm, hbm, hbm, pl.BlockSpec(memory_space=pltpu.SMEM), hbm, hbm],
        out_specs=vmem,
        scratch_shapes=[
            pltpu.VMEM((128, 192), bf16),
            pltpu.VMEM((8, 576), bf16),
            pltpu.VMEM((32, WIDE, BLK), bf16),
            pltpu.VMEM((MASK, 32 * BLK), bf16),
            pltpu.VMEM((16, 640), bf16),
            pltpu.VMEM((NX, 16, 640), bf16),
            pltpu.VMEM((640, BLK), bf16),
            pltpu.VMEM((192, 128), bf16),
            pltpu.VMEM((NZ, 192, 128), bf16),
            pltpu.VMEM((ROWS, 640), bf16),
            pltpu.VMEM((ROWS, 128), f32),
            pltpu.VMEM((16, 128, LAT), bf16),
            pltpu.VMEM((16, LAT, 128), bf16),
            pltpu.VMEM((HALF, 640), f32),
            pltpu.VMEM((HALF, 640), f32),
            pltpu.VMEM((HALF, 640), bf16),
            pltpu.VMEM((HALF, 640), bf16),
            pltpu.VMEM((HALF, 128), f32),
            pltpu.VMEM((ROWS, 128), f32),
            pltpu.VMEM((ROWS, 128), f32),
            pltpu.VMEM((4, ROWS, 128), f32),
            pltpu.VMEM((ROWS, 128), f32),
            pltpu.VMEM((NZ, 128, 128), bf16),
            pltpu.VMEM((NZ, 128, 128), bf16),
            pltpu.VMEM((NZ, 8, 128), f32),
            pltpu.VMEM((NZ, 8, 128), f32),
            dma((5,)),
            dma((5,)),
            dma((16, 2)),
            dma((8,)),
            dma((NZ,)),
            dma((1,)),
            dma((2,)),
            dma((1,)),
        ],
        compiler_params=pltpu.CompilerParams(
            collective_id=0, has_side_effects=True, vmem_limit_bytes=56 << 20
        ),
    )(queries.reshape(128, 192), cache.T, new_entries, cache_len, absorb_k, absorb_v)
    return out.reshape(8, 16, 128)


def solution(mesh):
    in_specs = (
        P("ctx", "head", None),
        P("head", None, None),
        P("head", None, None),
        P(("ctx", "head"), None),
        P("ctx", None),
        P(),
    )
    out_specs = P("ctx", "head", None)
    return jax.shard_map(body, mesh=mesh, in_specs=in_specs, out_specs=out_specs, check_vma=False)
```

```python
import math

import jax
import jax.numpy as jnp
from jax import lax
from jax.experimental import pallas as pl
from jax.experimental.pallas import tpu as pltpu
from jax.sharding import PartitionSpec as P

f32 = jnp.float32
bf16 = jnp.bfloat16
NEG = -1e30
LOG2E = 1.4426950408889634
MESH = pl.DeviceIdType.MESH

NZ, NX, NY = 8, 4, 4
BLK = 128
WIDE = 576
MASK = 64
LAT = 512
NEW_ROWS = 64
CH = 4 * BLK
HALF = 512
ROWS = 2 * HALF

NEAR = (0, 1, 7, 2)
FAR = (6, 3, 5, 4)
SPOT = {d: n for n, d in enumerate(NEAR + FAR)}

ORDER = [
    (0, 0, 0), (1, 0, 0), (0, 1, 0), (0, 2, 0),
    (0, 0, 1), (0, 0, 2), (1, 1, 0), (1, 2, 0),
    (1, 0, 1), (1, 0, 2), (0, 3, 0), (0, 0, 3),
    (0, 1, 1), (0, 1, 2), (0, 2, 1), (0, 2, 2),
    (1, 3, 0), (1, 0, 3), (1, 1, 1), (1, 1, 2),
    (1, 2, 1), (1, 2, 2), (0, 3, 1), (0, 3, 2),
    (0, 1, 3), (0, 2, 3), (1, 3, 1), (1, 3, 2),
    (1, 1, 3), (1, 2, 3), (0, 3, 3), (1, 3, 3),
]
PLACE = {b: n for n, b in enumerate(ORDER)}
OFFSET = (0, 3, 1, 2)

N, F = 0, 1
UNITS = [
    (N, 0), (N, 1), (F, 0), (F, 1), (N, 2), (F, 2), (F, 3), (F, 4),
    (F, 5), (F, 6), (F, 7), (N, 3), (N, 4), (N, 5), (N, 6), (N, 7),
]
PASS = {0: [(1, 0), (2, 0)], 1: [(0, 1), (0, 2)], 2: [(3, 0)], 3: [(1, 1), (1, 2), (0, 3)], 4: [(2, 1), (2, 2)], 5: [(3, 1), (3, 2)], 7: [(1, 3), (2, 3)], 8: [(3, 3)]}


def dot_t(a, b):
    return lax.dot_general(a, b, (((1,), (1,)), ((), ())), preferred_element_type=f32)


def dot_n(a, b):
    return jnp.dot(a, b, preferred_element_type=f32)


def kernel(
    scale, q_hbm, cache_hbm, new_hbm, len_ref, wk_hbm, wv_hbm, out_ref,
    q_ref, new_ref, kbuf, kbias, nsend, nbuf, newk, qsend, qrecv, qabs, qn, wk, wv, sa, sb, pa, pb, al, top, tot, acc, ob, osend, orecv, ssend, srecv,
    w_sem, send_sem, k_sem, s_sem, q_sem, n_sem, o_sem, t_sem,
):
    ctx = lax.axis_index("ctx")
    head = lax.axis_index("head")
    z, x = ctx // NX, ctx % NX
    y, c = head // 2, head % 2

    def at(zz, xx, yy, cc):
        return (zz * NX + xx, yy * 2 + cc)

    on_x, on_y = 1 - c, c
    ax1p = at(z, (x + on_x) % NX, (y + on_y) % NY, c)
    ax1m = at(z, (x + 3 * on_x) % NX, (y + 3 * on_y) % NY, c)
    ax2p = at(z, (x + on_y) % NX, (y + on_x) % NY, c)
    ax2m = at(z, (x + 3 * on_y) % NX, (y + 3 * on_x) % NY, c)
    sib = at(z, x, y, 1 - c)
    z_to = [None] + [at((z + d) % NZ, x, y, c) for d in range(1, NZ)]
    x_to = [None] + [at(z, (x + d) % NX, y, c) for d in range(1, NX)]

    barrier = pltpu.get_barrier_semaphore()
    partners = [ax1p, ax1m, ax2p, ax2m, sib, x_to[2]] + z_to[1:]
    for who in partners:
        pl.semaphore_signal(barrier, inc=1, device_id=who, device_id_type=MESH)
    pairs = [(q_hbm, q_ref), (new_hbm, new_ref), (cache_hbm, kbuf.at[0]), (wk_hbm, wk), (wv_hbm, wv)]
    loads = [pltpu.make_async_copy(src, dst, w_sem.at[n]) for n, (src, dst) in enumerate(pairs)]
    for load in loads:
        load.start()
    own_copy, wk_copy, wv_copy = loads[2:]
    for load in loads[:2]:
        load.wait()

    length = len_ref[0]
    qsend[0:128, :] = q_ref[:, 0:128]
    qsend[128:192, :] = jnp.concatenate([q_ref[0:64, 128:192], q_ref[64:128, 128:192]], axis=1)
    fresh = new_ref[...].astype(f32)
    fresh = jnp.concatenate([fresh, jnp.zeros((8, 576), f32)], axis=0)
    fresh = jnp.concatenate([fresh, jnp.zeros((16, 64), f32)], axis=1).astype(bf16)
    nbuf[0] = fresh
    nsend[...] = fresh

    pl.semaphore_wait(barrier, len(partners))

    def send(kind, src, dst, who, recv):
        pltpu.make_async_remote_copy(
            src_ref=src, dst_ref=dst, send_sem=send_sem.at[kind], recv_sem=recv, device_id=who, device_id_type=MESH
        ).start()

    def rows_of(block, half=None):
        ref = kbuf.at[PLACE[block]]
        return ref if half is None else ref.at[288 * half : 288 * half + 288]

    def k_send(block, to_block, who, half):
        _, d1, d2 = to_block
        src = cache_hbm.at[288 * half : 288 * half + 288] if block == (0, 0, 0) else rows_of(block, half)
        send(0, src, rows_of(to_block, half), who, k_sem.at[d1 * 4 + d2, half])

    def sib_send(d1, d2):
        block = (1, d1, d2)
        src = rows_of((0, d1, d2)) if d1 or d2 else cache_hbm
        send(0, src, rows_of(block), sib, s_sem.at[PLACE[block] // 4])

    def wait_at(ref, sem):
        pltpu.make_async_copy(ref, ref, sem).wait()

    def wait_sib(chunk):
        count = sum(b[0] for b in ORDER[4 * chunk : 4 * chunk + 4])
        if count:
            wait_at(kbuf.at[4 * chunk : 4 * chunk + count], s_sem.at[chunk])

    def half_event(d1, d2, half):
        block = (0, d1, d2)
        wait_at(rows_of(block, half), k_sem.at[d1 * 4 + d2, half])
        if d2 == 0:
            if d1 == 1 and half == 0:
                k_send(block, (0, 3, 0), ax1p, 0)
            if d1 == 2 and half == 1:
                k_send(block, (0, 3, 0), ax1m, 1)
            k_send(block, (0, d1, 1), ax2p, half)
            k_send(block, (0, d1, 2), ax2m, half)
        elif d2 == 1 and half == 0:
            k_send(block, (0, d1, 3), ax2p, 0)
        elif d2 == 2 and half == 1:
            k_send(block, (0, d1, 3), ax2m, 1)

    def event(*blocks):
        for turn in range(2):
            for d1, d2 in blocks:
                first = 1 if (d2 or d1) == 2 else 0
                half_event(d1, d2, first ^ turn)
        for d1, d2 in blocks:
            sib_send(d1, d2)

    def q_send(d, to, half=None, src=None):
        part = slice(0, 192) if half is None else slice(96 * half, 96 * half + 96)
        src = qsend if src is None else src
        send(1, src.at[part], qrecv.at[d, part], to, q_sem.at[d])

    for d in range(1, NX):
        send(2, nsend, nbuf.at[d], x_to[d], n_sem.at[0])
    q_send(1, z_to[1])
    q_send(7, z_to[7])
    q_send(2, z_to[2])
    q_send(6, z_to[6])
    own = (0, 0, 0)
    for turn in range(2):
        k_send(own, (0, 1, 0), ax1p, turn)
        k_send(own, (0, 2, 0), ax1m, 1 - turn)
    for turn in range(2):
        k_send(own, (0, 0, 1), ax2p, turn)
        k_send(own, (0, 0, 2), ax2m, 1 - turn)
    sib_send(0, 0)

    def place(d):
        r = slice(128 * SPOT[d], 128 * SPOT[d] + 128)
        lane64 = lax.broadcasted_iota(jnp.int32, (128, 64), 1)
        row_j = lax.broadcasted_iota(jnp.int32, (128, 64), 0) // 16
        block = qsend if d == 0 else qrecv.at[d]
        qn[r, :] = block[0:128, :].astype(f32)
        rope = block[128:192, :]
        rope = jnp.concatenate([rope[:, 0:64], rope[:, 64:128]], axis=0)
        pick = jnp.where(lane64 == d * 8 + row_j, 1.0, 0.0).astype(bf16)
        qabs[r, LAT:640] = jnp.concatenate([rope, pick], axis=1)

    def absorb(half):
        for h in range(16):
            part = qn[pl.ds(HALF * half + h, 32, stride=16), :].astype(bf16)
            lat = dot_n(part, wk[h])
            for n in range(4):
                acc[n, pl.ds(HALF * half + h, 32, stride=16), :] = lat[:, 128 * n : 128 * n + 128]
        for t in range(8):
            r = slice(HALF * half + 64 * t, HALF * half + 64 * t + 64)
            for n in range(4):
                qabs[r, 128 * n : 128 * n + 128] = acc[n, r, :].astype(bf16)

    def mask_slots(block):
        plane, d1, d2 = block
        first_x = on_x if plane == 0 else on_y
        s1, s2 = OFFSET[d1], OFFSET[d2]
        sx = (x + s1 * first_x + s2 * (1 - first_x)) % NX
        sy = (y + s1 * (1 - first_x) + s2 * first_x) % NY
        sc = c if plane == 0 else 1 - c
        slot = ((z * NX + sx) * NY + sy) * (2 * BLK) + sc * BLK
        here = PLACE[block] * BLK
        key = lax.broadcasted_iota(jnp.int32, (MASK, BLK), 1)
        kbias[:, here : here + BLK] = jnp.where(slot + key < length, 0.0, NEG).astype(bf16)

    def take_new():
        wait_at(nbuf.at[1:NX], n_sem.at[0])
        rows = [nbuf[d].astype(f32) for d in range(NX)] + [jnp.zeros((NEW_ROWS, 640), f32)]
        rows = jnp.concatenate(rows, axis=0)
        for n in range(5):
            newk[128 * n : 128 * n + 128, :] = rows[:, 128 * n : 128 * n + 128].T.astype(bf16)
        key = lax.broadcasted_iota(jnp.int32, (MASK, BLK), 1)
        row = lax.broadcasted_iota(jnp.int32, (MASK, BLK), 0)
        n_j = key % 16
        n_rank = n_j * (NZ * NX) + z * NX + (x + NX - key // 16) % NX
        q_rank = (row % 8) * (NZ * NX) + (z + NZ - row // 8) % NZ * NX + x
        seen = (key < NEW_ROWS) & (n_j < 8) & (n_rank <= q_rank)
        newk[WIDE : WIDE + MASK, :] = jnp.where(seen, 0.0, NEG).astype(bf16)

    def keys_of(b):
        both = jnp.concatenate([kbuf[b], kbuf[b + 1]], axis=1)
        return jnp.concatenate([both, kbias[:, BLK * b : BLK * b + 2 * BLK]], axis=0)

    def scores(unit, s):
        half, chunk = unit
        q = qabs.at[HALF * half : HALF * half + HALF]
        for lo in range(0, CH, 256):
            s[:, lo : lo + 256] = dot_n(q[...], keys_of(4 * chunk + lo // BLK))
        if chunk == 0:
            s[:, CH : CH + BLK] = dot_n(q[...], newk[...])

    def weigh(unit, s, p):
        half, chunk = unit
        size = CH + BLK if chunk == 0 else CH
        for t in range(HALF // 32):
            sr = slice(32 * t, 32 * t + 32)
            r = slice(HALF * half + 32 * t, HALF * half + 32 * t + 32)
            sc = s[sr, 0:size]
            new_top = jnp.broadcast_to(jnp.max(sc, axis=1, keepdims=True), (32, 128))
            if chunk:
                old_top = top[r, :]
                new_top = jnp.maximum(old_top, new_top)
                shrink = jnp.exp2((old_top - new_top) * scale)
                al[sr, :] = shrink
            top[r, :] = new_top
            w = jnp.exp2((sc - new_top[:, 0:1]) * scale)
            part = w[:, 0:128]
            for lo in range(128, size, 128):
                part = part + w[:, lo : lo + 128]
            if chunk:
                part = part + tot[r, :] * shrink
            tot[r, :] = part
            p[sr, 0:size] = w.astype(bf16)

    def mix(unit, p):
        half, chunk = unit
        size = CH + BLK if chunk == 0 else CH
        for n in range(2):
            cols = slice(256 * n, 256 * n + 256)
            v = [kbuf[chunk * 4 + b, cols, :] for b in range(4)]
            if chunk == 0:
                v = v + [newk[cols, :]]
            v = jnp.concatenate(v, axis=1)
            for t in range(HALF // 256):
                sr = slice(256 * t, 256 * t + 256)
                r = slice(HALF * half + 256 * t, HALF * half + 256 * t + 256)
                o = dot_t(p[sr, 0:size], v)
                for k in range(2):
                    part = o[:, 128 * k : 128 * k + 128]
                    m = 2 * n + k
                    acc[m, r, :] = part if chunk == 0 else acc[m, r, :] * al[sr, :] + part

    def deliver(half):
        lane = lax.broadcasted_iota(jnp.int32, (128, 128), 1)
        owners = NEAR if half == N else FAR
        for d in owners:
            r = slice(128 * SPOT[d], 128 * SPOT[d] + 128)
            total = jnp.sum(tot[r, :], axis=1, keepdims=True)
            ssend[d] = jnp.where(lane == 0, top[r, :], total).T[0:8, :]
            if d:
                send(3, ssend.at[d], srecv.at[d], z_to[NZ - d], t_sem.at[0])
        for h in range(16):
            rows = pl.ds(HALF * half + h, 32, stride=16)
            part = jnp.concatenate([acc[n, rows, :] for n in range(4)], axis=1)
            hi = part.astype(bf16)
            lo = (part - hi.astype(f32)).astype(bf16)
            both = dot_n(jnp.concatenate([hi, lo], axis=0), wv[h])
            ob[rows, :] = both[0:32] + both[32:64]
        for d in owners:
            if d:
                osend[d] = ob[128 * SPOT[d] : 128 * SPOT[d] + 128, :].astype(bf16)
                send(4, osend.at[d], orecv.at[d], z_to[NZ - d], o_sem.at[half])

    def relay():
        wait_at(qrecv.at[2], q_sem.at[2])
        q_send(3, z_to[1], src=qrecv.at[2])
        q_send(4, z_to[2], half=0, src=qrecv.at[2])
        wait_at(qrecv.at[6], q_sem.at[6])
        q_send(5, z_to[7], src=qrecv.at[6])
        q_send(4, z_to[6], half=1, src=qrecv.at[6])

    def take_near():
        wait_at(qrecv.at[1], q_sem.at[1])
        wait_at(qrecv.at[7], q_sem.at[7])
        for d in NEAR[1:]:
            place(d)

    def take_far():
        wait_at(qrecv.at[3], q_sem.at[3])
        wait_at(qrecv.at[5], q_sem.at[5])
        wait_at(qrecv.at[4], q_sem.at[4])
        for d in FAR:
            place(d)

    ready = set()
    sib_in = set()

    def before(n):
        half, chunk = UNITS[n]
        if n == 0:
            relay()
        event(*PASS.get(n, ()))
        if n == 0:
            take_near()
            wk_copy.wait()
            absorb(N)
        if (half, chunk) == (F, 0):
            take_far()
            absorb(F)
        if n == 0:
            own_copy.wait()
        if chunk in ready:
            return
        ready.add(chunk)
        wait_sib(chunk)

    place(0)
    for b in ORDER:
        mask_slots(b)
    take_new()
    before(0)
    scores(UNITS[0], sa)
    for n, unit in enumerate(UNITS):
        s_now, s_next, p = (sa, sb, pa) if n % 2 == 0 else (sb, sa, pb)
        if n + 1 < len(UNITS):
            before(n + 1)
            scores(UNITS[n + 1], s_next)
        weigh(unit, s_now, p)
        mix(unit, p)
        if unit == (F, 7):
            wv_copy.wait()
            deliver(F)
    deliver(N)

    wait_at(srecv.at[1:NZ], t_sem.at[0])
    tops = [ssend[0, 0:1, :]] + [srecv[d, 0:1, :] for d in range(1, NZ)]
    totals = [ssend[0, 1:2, :]] + [srecv[d, 1:2, :] for d in range(1, NZ)]
    best = tops[0]
    for d in range(1, NZ):
        best = jnp.maximum(best, tops[d])
    shares = [jnp.exp2((t - best) * scale) for t in tops]
    full = shares[0] * totals[0]
    for d in range(1, NZ):
        full = full + shares[d] * totals[d]
    shares = [s / full for s in shares]
    by_row = jnp.concatenate(shares + [jnp.zeros((120, 128), f32)], axis=0).T
    result = ob[0:128, :] * by_row[:, 0:1]
    wait_at(orecv.at[0:4], o_sem.at[F])
    for d in FAR + NEAR[1:]:
        if d == NEAR[1]:
            wait_at(orecv.at[0:3], o_sem.at[N])
        result = result + orecv[d].astype(f32) * by_row[:, d : d + 1]
    out_ref[...] = result.astype(bf16)
    for kind, ref in enumerate((kbuf.at[0:31], qrecv.at[0:7], nbuf.at[0:3], ssend.at[0:7], osend.at[0:7])):
        wait_at(ref, send_sem.at[kind])


def body(queries, absorb_k, absorb_v, cache, new_entries, cache_len):
    scale = LOG2E / math.sqrt(queries.shape[2])
    vmem = pl.BlockSpec(memory_space=pltpu.VMEM)
    hbm = pl.BlockSpec(memory_space=pl.ANY)
    dma = pltpu.SemaphoreType.DMA

    def run(*refs):
        kernel(scale, *refs)

    out = pl.pallas_call(
        run,
        out_shape=jax.ShapeDtypeStruct((128, 128), bf16),
        in_specs=[hbm, hbm, hbm, pl.BlockSpec(memory_space=pltpu.SMEM), hbm, hbm],
        out_specs=vmem,
        scratch_shapes=[
            pltpu.VMEM((128, 192), bf16),
            pltpu.VMEM((8, 576), bf16),
            pltpu.VMEM((32, WIDE, BLK), bf16),
            pltpu.VMEM((MASK, 32 * BLK), bf16),
            pltpu.VMEM((16, 640), bf16),
            pltpu.VMEM((NX, 16, 640), bf16),
            pltpu.VMEM((640, BLK), bf16),
            pltpu.VMEM((192, 128), bf16),
            pltpu.VMEM((NZ, 192, 128), bf16),
            pltpu.VMEM((ROWS, 640), bf16),
            pltpu.VMEM((ROWS, 128), f32),
            pltpu.VMEM((16, 128, LAT), bf16),
            pltpu.VMEM((16, LAT, 128), bf16),
            pltpu.VMEM((HALF, 640), f32),
            pltpu.VMEM((HALF, 640), f32),
            pltpu.VMEM((HALF, 640), bf16),
            pltpu.VMEM((HALF, 640), bf16),
            pltpu.VMEM((HALF, 128), f32),
            pltpu.VMEM((ROWS, 128), f32),
            pltpu.VMEM((ROWS, 128), f32),
            pltpu.VMEM((4, ROWS, 128), f32),
            pltpu.VMEM((ROWS, 128), f32),
            pltpu.VMEM((NZ, 128, 128), bf16),
            pltpu.VMEM((NZ, 128, 128), bf16),
            pltpu.VMEM((NZ, 8, 128), f32),
            pltpu.VMEM((NZ, 8, 128), f32),
            dma((5,)),
            dma((5,)),
            dma((16, 2)),
            dma((8,)),
            dma((NZ,)),
            dma((1,)),
            dma((2,)),
            dma((1,)),
        ],
        compiler_params=pltpu.CompilerParams(
            collective_id=0, has_side_effects=True, vmem_limit_bytes=56 << 20
        ),
    )(queries.reshape(128, 192), cache.T, new_entries, cache_len, absorb_k, absorb_v)
    return out.reshape(8, 16, 128)


def solution(mesh):
    in_specs = (
        P("ctx", "head", None),
        P("head", None, None),
        P("head", None, None),
        P(("ctx", "head"), None),
        P("ctx", None),
        P(),
    )
    out_specs = P("ctx", "head", None)
    return jax.shard_map(body, mesh=mesh, in_specs=in_specs, out_specs=out_specs, check_vma=False)
```
